256 devices in a mesh: lon: 4 (over x), lat: 4 (over y), lev: 16 (over z, core).
Axes of the slice: x: 4, y: 4, z: 8, core: 2. Of those that a mesh axis runs over, the one named last changes fastest.
Arguments:
- control: float32 [6, 48, 256, 512], P(None, 'lev', 'lat', 'lon'), may hold values from -6 to 6
- vertical: float32 [6, 48, 48], replicated, may hold values from -0.875 to 0.875
- lon_taps: float32 [6, 48, 31], P(None, 'lev'), may hold values from 0.03 to 0.12
- lat_taps: float32 [6, 48, 31], P(None, 'lev'), may hold values from 0.03 to 0.12
- innovation: float32 [6, 48, 8192], P(None, 'lev', ('lon', 'lat')), may hold values from -12 to 12
- inv_variance: float32 [6, 48], P(None, 'lev'), may hold values from 0.5 to 2
- obs_tile: int32 [8192], P(('lon', 'lat')), may hold values from 0 to 15, as said below
- obs_cell: int32 [8192], P(('lon', 'lat')), may hold values from 0 to 8191
Outputs:
- gradient: float32 [6, 48, 256, 512], P(None, 'lev', 'lat', 'lon')
The draws below stay inside these ranges and needn't reach their ends.
Inputs may be any that keep to these rules, and one draw needn't show every extreme that they name: `obs_tile`: the rows of one source device name each tile at most 64 times, and one tile is named exactly 64 times by the rows of every source device.
All inputs are finite; a program needn't handle non-finite values.
Results may differ from the reference program's by a relative error of at most 0.00005.
Values sent between devices are 32-bit elements; how exact they have to be, the bound alone decides.
No kernel may reach another device: no remote copies, remote signals or barrier semaphores. Data moves between devices by JAX's collectives and lax.ppermute only.
A program may use at most 64 MiB of HBM per device.

```python
import math
import jax
import jax.numpy as jnp
from jax import lax

NV = 6
LEV = 48
TAPS = 31
CX = 128
CY = 64
OBS_DEV = 512
NLON = 512
NLAT = 256
TILE_TOTAL = 16
MAX_TILE_ROWS = 64
OBS_ROWS = 8192
N_LAT = 4


def draw_obs_tile(key, part):
    key = jax.random.fold_in(key, 7)
    tile_random_key, hot_key, row_key = jax.random.split(key, 3)
    extra_credit = jax.random.randint(tile_random_key, (TILE_TOTAL,), 0, 4)
    hot_tile = jax.random.randint(hot_key, (), 0, TILE_TOTAL)
    slot_numbers = jnp.arange(TILE_TOTAL * MAX_TILE_ROWS, dtype=jnp.int32)
    tile_of_slot = slot_numbers // MAX_TILE_ROWS

    def one_source(source_key):
        ranking_key, order_key = jax.random.split(source_key)
        tile_scores = (jax.random.randint(ranking_key, (TILE_TOTAL * MAX_TILE_ROWS,), 0, 4096) + extra_credit[tile_of_slot] * 1024) * (TILE_TOTAL * MAX_TILE_ROWS) + slot_numbers
        tile_scores = tile_scores + jnp.where(tile_of_slot == hot_tile, 2 ** 28, 0)
        chosen = lax.top_k(tile_scores, OBS_DEV)[1]
        chosen = jax.random.permutation(order_key, chosen)
        return (chosen // MAX_TILE_ROWS).astype(jnp.int32)
    owners = jax.vmap(one_source)(jax.random.split(row_key, TILE_TOTAL))
    return owners.reshape(-1).astype(jnp.int32)


def touch_ends(entries, stream_key, smallest, high):
    index_at = [jax.random.randint(jax.random.fold_in(stream_key, axis), (), 0, length) for axis, length in enumerate(entries.shape)]
    longest = entries.shape.index(max(entries.shape))
    neighbour = index_at[:longest] + [(index_at[longest] + 1) % entries.shape[longest]] + index_at[longest + 1:]
    return entries.at[tuple(index_at)].set(smallest).at[tuple(neighbour)].set(high)


def block_scale(own_key, dims, cuts, low, largest):
    gain, own = 1.0, jax.random.fold_in(own_key, 6)
    for dim, blocks in cuts:
        draws = jnp.exp(jax.random.uniform(jax.random.fold_in(own, dim), (blocks,), jnp.float32, low / len(cuts), largest / len(cuts)))
        gain = gain * jnp.repeat(draws, dims[dim] // blocks).reshape([-1 if axis == dim else 1 for axis in range(len(dims))])
    return gain


def scatter_about(key, shape, deviation, limit, cuts=(), kind=jnp.bfloat16):
    factor_of = block_scale(key, shape, cuts, -0.22, 0.18) if cuts else 1.0
    drawn = jax.random.normal(key, shape, jnp.float32) * deviation * factor_of
    return jnp.minimum(jnp.maximum(drawn, -limit), limit).astype(kind)


def setup_inputs(seed: int = 0) -> dict:
    key_of = jax.random.split(jax.random.key(seed), 9)
    control = scatter_about(key_of[0], (NV, LEV, NLAT, NLON), 1.0, 6.0, ((1, 16), (2, 4), (3, 4)), jnp.float32)
    vertical = scatter_about(key_of[1], (NV, LEV, LEV), LEV ** -0.5, 0.875, (), jnp.float32)
    lon_taps = jnp.clip(0.03 + 0.089999998 * jax.random.uniform(key_of[2], (NV, LEV, TAPS), jnp.float32) ** block_scale(key_of[2], (NV, LEV, TAPS), ((1, 16),), -0.2, 0.2), 0.03, 0.12)
    lat_taps = jnp.clip(0.03 + 0.089999998 * jax.random.uniform(key_of[3], (NV, LEV, TAPS), jnp.float32) ** block_scale(key_of[3], (NV, LEV, TAPS), ((1, 16),), -0.2, 0.2), 0.03, 0.12)
    innovation = scatter_about(key_of[4], (NV, LEV, OBS_ROWS), 2.0, 12.0, ((1, 16), (2, 16)), jnp.float32)
    inv_variance = jnp.clip(jnp.exp(math.log(2.0) - 1.3862944 * jax.random.uniform(key_of[5], (NV, LEV), jnp.float32) ** block_scale(key_of[5], (NV, LEV), ((1, 16),), -0.2, 0.2)), 0.5, 2.0)
    obs_tile = draw_obs_tile(jax.random.fold_in(key_of[8], 71), 0)
    obs_cell = touch_ends(jax.random.randint(key_of[7], (OBS_ROWS,), 0, CX * CY), jax.random.fold_in(key_of[7], 1), 0, (CX * CY) - 1).astype(jnp.int32)
    return {"control": control, "vertical": vertical, "lon_taps": lon_taps, "lat_taps": lat_taps, "innovation": innovation, "inv_variance": inv_variance, "obs_tile": obs_tile, "obs_cell": obs_cell}


def shift_sum(grid_field, coeffs, axis, mode):
    count = coeffs.shape[1]
    reach = (count - 1) // 2
    pads = [(0, 0)] * grid_field.ndim
    pads[axis] = (reach, reach)
    padded = jnp.pad(grid_field, pads, mode=mode)
    extent = grid_field.shape[axis]
    summed = coeffs[:, 0][:, None, None] * lax.slice_in_dim(padded, 0, extent, axis=axis)
    for offset in range(1, count):
        summed = summed + coeffs[:, offset][:, None, None] * lax.slice_in_dim(padded, offset, offset + extent, axis=axis)
    return summed


def reference(control, vertical, lon_taps, lat_taps, innovation, inv_variance, obs_tile, obs_cell):
    lat_index = (obs_tile % N_LAT) * CY + obs_cell // CX
    lon_index = (obs_tile // N_LAT) * CX + obs_cell % CX

    def per_variable(packed):
        grid_field, matrix, lon_coeffs, lat_coeffs, observed, weights = packed
        first = jnp.einsum("kl,lyx->kyx", matrix, grid_field, precision=lax.Precision.HIGHEST)
        second = shift_sum(first, lon_coeffs, 2, "wrap")
        third = shift_sum(second, lat_coeffs, 1, "constant")
        picked = third[:, lat_index, lon_index]
        misfit = (picked - observed) * weights[:, None]
        placed = jnp.zeros_like(third).at[:, lat_index, lon_index].add(misfit)
        back_lat = shift_sum(placed, lat_coeffs[:, ::-1], 1, "constant")
        back_lon = shift_sum(back_lat, lon_coeffs[:, ::-1], 2, "wrap")
        return grid_field + jnp.einsum("lk,lyx->kyx", matrix, back_lon, precision=lax.Precision.HIGHEST)

    return lax.map(per_variable, (control, vertical, lon_taps, lat_taps, innovation, inv_variance))
```

```python
import functools

import jax
import jax.numpy as jnp
from jax import lax
from jax.experimental import pallas as pl
from jax.experimental.pallas import tpu as pltpu
from jax.sharding import PartitionSpec as P

F32, BF16, I32 = jnp.float32, jnp.bfloat16, jnp.int32
ROWS, COLS = 64, 128
TAPS = 31
STRIP = 16
LEVELS = 48
RINGS = 8
OWN = 6
SLOTS = 64
TILES = 16
VMEM = pl.BlockSpec(memory_space=pltpu.VMEM)
SMEM = pl.BlockSpec(memory_space=pltpu.SMEM)


def kernel_call(body, outs, ins, scratch=(), smem=(), flops=0, limit=40):
    moved = sum(a.size * a.dtype.itemsize for a in ins)
    moved += sum(o.size * o.dtype.itemsize for o in outs)
    return pl.pallas_call(
        body,
        out_shape=list(outs),
        in_specs=[SMEM if i in smem else VMEM for i in range(len(ins))],
        out_specs=[VMEM] * len(outs),
        scratch_shapes=list(scratch),
        compiler_params=pltpu.CompilerParams(vmem_limit_bytes=limit * 2**20),
        cost_estimate=pl.CostEstimate(flops=flops, bytes_accessed=moved, transcendentals=0),
    )(*ins)


def shape(*dims, dtype=F32):
    return jax.ShapeDtypeStruct(dims, dtype)


def split(value):
    high = value.astype(BF16)
    return high, (value - high.astype(F32)).astype(BF16)


def mm(a, b):
    return jnp.dot(a, b, preferred_element_type=F32)


def mm_nt(a, b):
    return lax.dot_general(a, b, (((1,), (1,)), ((), ())), preferred_element_type=F32)


def arrange_body(nv, core, control, mate, out):
    c = core[0]
    for v in range(nv):
        for l in range(3):
            out[:, v * 3 + l] = control[c * nv + v, l].reshape(RINGS, 8, COLS)
            out[:, nv * 3 + v * 3 + l] = mate[v * 3 + l].reshape(RINGS, 8, COLS)


def arrange(core, control, mate):
    nv = control.shape[0] // 2
    return kernel_call(
        functools.partial(arrange_body, nv),
        [shape(RINGS, 6 * nv, 8, COLS)],
        [core, control, mate],
        smem=(0,),
    )[0]


def rows_of(v, start, count):
    return pl.ds(v * LEVELS * 8 + start, count)


def mixed(matrix, held, v):
    at = [pl.ds(v * LEVELS * 8 + s, LEVELS, stride=8) for s in range(8)]
    columns = jnp.concatenate([held[a, :] for a in at], axis=1)
    result = jnp.dot(
        matrix[v], columns, precision=lax.Precision.HIGHEST, preferred_element_type=F32
    )
    for s in range(8):
        held[at[s], :] = result[:, s * COLS : (s + 1) * COLS]


def mix_body(nv, got, matrix, out, held):
    for v in range(nv):
        for s in range(RINGS):
            for t in range(2):
                first = t * 3 * nv + v * 3
                held[rows_of(v, (s * 2 + t) * 24, 24), :] = got[s, first : first + 3].reshape(24, COLS)
        mixed(matrix, held, v)
        for s in range(RINGS):
            out[s, v * OWN : (v + 1) * OWN] = held[rows_of(v, s * 48, 48), :].reshape(OWN, 8, COLS)


def unmix_body(nv, got, matrix, control, out, held):
    for v in range(nv):
        for s in range(RINGS):
            held[rows_of(v, s * 48, 48), :] = got[s, v * OWN : (v + 1) * OWN].reshape(48, COLS)
        mixed(matrix, held, v)
        for s in range(RINGS):
            for t in range(2):
                first = t * 3 * nv + v * 3
                part = held[rows_of(v, (s * 2 + t) * 24, 24), :].reshape(3, 8, COLS)
                out[s, first : first + 3] = part + control[s, first : first + 3]


def mix(got, matrix):
    nv = matrix.shape[0]
    return kernel_call(
        functools.partial(mix_body, nv),
        [shape(*got.shape)],
        [got, matrix],
        scratch=[pltpu.VMEM((nv * LEVELS * 8, COLS), F32)],
        flops=2 * nv * LEVELS * LEVELS * 1024 * 6,
    )[0]


def unmix(got, matrix, control):
    nv = matrix.shape[0]
    return kernel_call(
        functools.partial(unmix_body, nv),
        [shape(*got.shape)],
        [got, matrix, control],
        scratch=[pltpu.VMEM((nv * LEVELS * 8, COLS), F32)],
        flops=2 * nv * LEVELS * LEVELS * 1024 * 6,
    )[0]


def bands_body(planes, taps, lat_high, lat_low, lon_high, lon_low):
    def one(p, carry):
        for flip in range(2):
            lat = jnp.broadcast_to(taps[flip, p, :, 0:128], (ROWS, 128))
            lat = pltpu.roll(lat, 128 - 15, 1, stride=1, stride_axis=0)
            lat_high[flip, p], lat_low[flip, p] = split(lat)
            lon = jnp.broadcast_to(taps[flip, p, :, 128:384], (COLS, 256))
            lon = pltpu.roll(lon, 256 - 15, 1, stride=1, stride_axis=0)
            lon_high[flip, p], lon_low[flip, p] = split(lon)
        return carry

    lax.fori_loop(0, planes, one, 0)


def bands(lon_taps, lat_taps):
    planes = lon_taps.shape[0]
    both = []
    for lon, lat in ((lon_taps, lat_taps), (lon_taps[:, ::-1], lat_taps[:, ::-1])):
        lat = jnp.pad(lat, ((0, 0), (0, 128 - TAPS)))
        lon = jnp.pad(lon, ((0, 0), (0, 256 - TAPS)))
        both.append(jnp.concatenate([lat, lon], axis=1))
    taps = jnp.stack(both)[:, :, None, :]
    return kernel_call(
        functools.partial(bands_body, planes),
        [shape(2, planes, ROWS, 128, dtype=BF16)] * 2 + [shape(2, planes, COLS, 256, dtype=BF16)] * 2,
        [taps],
        flops=planes * 200000,
    )


def lat_filter(p, rows, before, after, high, low):
    extended = jnp.concatenate(
        [rows[:, p].reshape(ROWS, COLS), after[:, p].reshape(STRIP, COLS)]
        + [jnp.zeros((32, COLS), F32), before[:, p].reshape(STRIP, COLS)],
        axis=0,
    )
    e_high, e_low = split(extended)
    return mm(high[0, p], e_high) + (mm(high[0, p], e_low) + mm(low[0, p], e_high))


def lon_filter(p, l, field, left, right, high, low):
    lane = lax.broadcasted_iota(I32, (ROWS, COLS), 1)
    left = pltpu.roll(left, (COLS - STRIP - STRIP * l) % COLS, 1)
    right = pltpu.roll(right, (COLS - STRIP * l) % COLS, 1)
    halo = jnp.where(lane >= COLS - STRIP, left, jnp.where(lane < STRIP, right, 0.0))
    x_high, x_low = split(jnp.concatenate([field, halo], axis=1))
    return mm_nt(x_high, high[0, p]) + (mm_nt(x_low, high[0, p]) + mm_nt(x_high, low[0, p]))


def packed(fields):
    lane = lax.broadcasted_iota(I32, (ROWS, COLS), 1) // STRIP
    last = jnp.zeros((ROWS, COLS), F32)
    first = jnp.zeros((ROWS, COLS), F32)
    for l, field in enumerate(fields):
        last = jnp.where(lane == l, pltpu.roll(field, STRIP * (l + 1) % COLS, 1), last)
        first = jnp.where(lane == l, pltpu.roll(field, STRIP * l, 1) if l else field, first)
    return last, first


def lat_body(nv, rows, before, after, high, low, out, last, first):
    def one(v, carry):
        fields = [lat_filter(v * OWN + l, rows, before, after, high, low) for l in range(OWN)]
        for l in range(OWN):
            out[v * OWN + l] = fields[l]
        last[v], first[v] = packed(fields)
        return carry

    lax.fori_loop(0, nv, one, 0)


def back_lat_body(nv, rows, before, after, high, low, out):
    def one(v, carry):
        for l in range(OWN):
            p = v * OWN + l
            out[:, p] = lat_filter(p, rows, before, after, high, low).reshape(RINGS, 8, COLS)
        return carry

    lax.fori_loop(0, nv, one, 0)


def back_lon_body(nv, field, left, right, high, low, out):
    def one(v, carry):
        for l in range(OWN):
            p = v * OWN + l
            value = lon_filter(p, l, field[p], left[v], right[v], high, low)
            out[:, p] = value.reshape(RINGS, 8, COLS)
        return carry

    lax.fori_loop(0, nv, one, 0)


def observe_body(
    nv, field, left, right, high, low, values, weight, row_hot, row_hot16, col_hot, col_hot2,
    out, last, first, parts, picked, misfit_high, misfit_low,
):
    def filtered(v, carry):
        for l in range(OWN):
            p = v * OWN + l
            third = lon_filter(p, l, field[p], left[v], right[v], high, low)
            t_high, t_low = split(third)
            parts[p] = jnp.concatenate([t_high, t_low], axis=1)
        return carry

    lax.fori_loop(0, nv, filtered, 0)

    def gathered(v, carry):
        for l in range(OWN):
            p = v * OWN + l
            across = mm(parts[p], col_hot2[...])
            found = jnp.sum(across * row_hot[...], axis=0, keepdims=True)
            misfit = (found - values[p]) * weight[p]
            m_high, m_low = split(misfit)
            misfit_high[p] = m_high.astype(F32)
            misfit_low[p] = m_low.astype(F32)
        return carry

    lax.fori_loop(0, nv, gathered, 0)

    def scattered(v, carry):
        fields = []
        for l in range(OWN):
            p = v * OWN + l
            w_high = (row_hot[...] * misfit_high[p]).astype(BF16)
            w_low = (row_hot[...] * misfit_low[p]).astype(BF16)
            both = mm_nt(jnp.concatenate([w_high, w_low], axis=0), col_hot[...])
            fields.append(both[:ROWS] + both[ROWS:])
            out[p] = fields[-1]
        last[v], first[v] = packed(fields)
        return carry

    lax.fori_loop(0, nv, scattered, 0)


def route_body(innovation, tile, cell, out):
    count = tile.shape[1]
    hot = (lax.broadcasted_iota(I32, (TILES, count), 0) == tile[...]).astype(F32)
    earlier = lax.broadcasted_iota(I32, (count, count), 0) < lax.broadcasted_iota(I32, (count, count), 1)
    before = mm(hot.astype(BF16), earlier.astype(F32).astype(BF16))
    place = jnp.sum(before * hot, axis=0, keepdims=True).astype(I32)
    slot = tile[...] * SLOTS + place
    slot_hot = (lax.broadcasted_iota(I32, (TILES * SLOTS, count), 0) == slot).astype(F32).astype(BF16)
    sent = jnp.concatenate(
        [innovation[...], (cell[...] + 1).astype(F32), jnp.zeros((5, count), F32)], axis=0
    )
    high, rest = split(sent)
    remainder = sent - high.astype(F32)
    low = (remainder - rest.astype(F32)).astype(BF16)
    all_parts = mm_nt(jnp.concatenate([high, rest, low], axis=0), slot_hot)
    full = all_parts[0:24] + (all_parts[24:48] + all_parts[48:72])
    lane = lax.broadcasted_iota(I32, (8, COLS), 1)
    for e in range(TILES // 2):
        at = slice(e * COLS, (e + 1) * COLS)
        a, b, c = full[0:8, at], full[8:16, at], full[16:24, at]
        a2, b2, c2 = [pltpu.roll(x, SLOTS, 1) for x in (a, b, c)]
        out[2 * e, 0:8] = jnp.where(lane < SLOTS, a, b2)
        out[2 * e, 8:16] = jnp.where(lane < SLOTS, c, 0.0)
        out[2 * e + 1, 0:8] = jnp.where(lane < SLOTS, a2, b)
        out[2 * e + 1, 8:16] = jnp.where(lane < SLOTS, c2, 0.0)


def arrived_body(got, values, row_hot, row_hot16, col_hot, col_hot2):
    lane = lax.broadcasted_iota(I32, (8, COLS), 1)
    full = []
    for e in range(TILES // 2):
        a, b = got[2 * e, 0:8], got[2 * e + 1, 0:8]
        c, d = got[2 * e, 8:16], got[2 * e + 1, 8:16]
        low = lane < SLOTS
        full.append(
            jnp.concatenate(
                [
                    jnp.where(low, a, pltpu.roll(b, SLOTS, 1)),
                    jnp.where(low, pltpu.roll(a, SLOTS, 1), b),
                    jnp.where(low, c, pltpu.roll(d, SLOTS, 1)),
                ],
                axis=0,
            )
        )
    full = jnp.concatenate(full, axis=1)
    for p in range(18):
        values[p] = full[p : p + 1]
    cell = full[18:19].astype(I32) - 1
    count = cell.shape[1]
    rows = (lax.broadcasted_iota(I32, (ROWS, count), 0) == (cell >> 7)).astype(F32)
    row_hot[...] = rows
    row_hot16[...] = rows.astype(BF16)
    cols = (lax.broadcasted_iota(I32, (COLS, count), 0) == (cell & 127)).astype(F32).astype(BF16)
    col_hot[...] = cols
    col_hot2[...] = jnp.concatenate([cols, cols], axis=0)


def neighbours(axis, wrap):
    size = lax.axis_size(axis)
    up = [(i, (i + 1) % size) for i in range(size if wrap else size - 1)]
    return up, [(j, i) for i, j in up]


def exchanged(last, first, axis, wrap):
    up, down = neighbours(axis, wrap)
    return lax.ppermute(last, axis, up), lax.ppermute(first, axis, down)


def with_mate(value):
    pairs = [(i, i ^ 1) for i in range(lax.axis_size("lev"))]
    return lax.ppermute(value, "lev", pairs)


def over_rings(value):
    size = lax.axis_size("lev")
    groups = [list(range(0, size, 2)), list(range(1, size, 2))]
    return lax.all_to_all(value, "lev", 0, 0, tiled=True, axis_index_groups=groups)


def local(control, vertical, lon_taps, lat_taps, innovation, inv_variance, obs_tile, obs_cell):
    core = lax.axis_index("lev") % 2
    core_ref = core.astype(I32).reshape(1)
    rows = obs_tile.shape[0]

    def half(value, which):
        return lax.dynamic_slice_in_dim(value, which * 3, 3, 0)

    small = jnp.concatenate(
        [innovation, lon_taps, lat_taps, inv_variance[:, :, None]], axis=2
    )
    mate_control = with_mate(half(control, 1 - core).reshape(9, ROWS, COLS))
    columns = over_rings(arrange(core_ref, control, mate_control))

    mate_small = with_mate(half(small, 1 - core))
    kept = half(small, core)
    natural = jnp.where(
        core == 0,
        jnp.concatenate([kept, mate_small], axis=1),
        jnp.concatenate([mate_small, kept], axis=1),
    ).reshape(18, -1)
    values = natural[:, :rows]
    lon18 = natural[:, rows : rows + TAPS]
    lat18 = natural[:, rows + TAPS : rows + 2 * TAPS]
    weight = natural[:, rows + 2 * TAPS]
    lat_high, lat_low, lon_high, lon_low = bands(lon18, lat18)

    matrix = half(vertical, core).reshape(3, LEVELS, RINGS, 2, 3)
    matrix = jnp.where(core == 0, matrix, matrix[:, :, :, ::-1]).reshape(3, LEVELS, LEVELS)
    flipped = jnp.swapaxes(matrix, 1, 2)

    routed = kernel_call(
        route_body,
        [shape(TILES, 16, COLS)],
        [values, obs_tile.reshape(1, -1), obs_cell.reshape(1, -1)],
        flops=2 * 72 * 1024 * rows,
    )[0]
    got_rows = lax.all_to_all(routed, ("lon", "lat"), 0, 0, tiled=True)
    slots = TILES * SLOTS
    obs, row_hot, row_hot16, col_hot, col_hot2 = kernel_call(
        arrived_body,
        [
            shape(18, 1, slots),
            shape(ROWS, slots),
            shape(ROWS, slots, dtype=BF16),
            shape(COLS, slots, dtype=BF16),
            shape(2 * COLS, slots, dtype=BF16),
        ],
        [got_rows],
        flops=1000000,
    )

    first = over_rings(mix(columns, matrix))
    nv = 3
    planes = nv * OWN
    before, after = exchanged(first[6:8], first[0:2], "lat", False)
    field_shape = shape(planes, ROWS, COLS)
    pack_shape = shape(nv, ROWS, COLS)
    lat_flops = 2 * 3 * planes * ROWS * 128 * COLS
    field, last, lead = kernel_call(
        functools.partial(lat_body, nv),
        [field_shape, pack_shape, pack_shape],
        [first, before, after, lat_high[0:1], lat_low[0:1]],
        flops=lat_flops,
    )
    left, right = exchanged(last, lead, "lon", True)
    placed, last, lead = kernel_call(
        functools.partial(observe_body, nv),
        [field_shape, pack_shape, pack_shape],
        [field, left, right, lon_high[0:1], lon_low[0:1], obs, weight, row_hot, row_hot16, col_hot, col_hot2],
        scratch=[
            pltpu.VMEM((planes, ROWS, 2 * COLS), BF16),
            pltpu.VMEM((planes, 1, slots), F32),
            pltpu.VMEM((planes, 1, slots), F32),
            pltpu.VMEM((planes, 1, slots), F32),
        ],
        smem=(6,),
        flops=2 * planes * ROWS * slots * 256 * 2,
    )
    left, right = exchanged(last, lead, "lon", True)
    back = kernel_call(
        functools.partial(back_lon_body, nv),
        [shape(RINGS, planes, 8, COLS)],
        [placed, left, right, lon_high[1:2], lon_low[1:2]],
        flops=2 * lat_flops,
    )[0]
    before, after = exchanged(back[6:8], back[0:2], "lat", False)
    back = kernel_call(
        functools.partial(back_lat_body, nv),
        [shape(RINGS, planes, 8, COLS)],
        [back, before, after, lat_high[1:2], lat_low[1:2]],
        flops=lat_flops,
    )[0]
    result = over_rings(unmix(over_rings(back), flipped, columns))

    mine, other = result[:, :9], with_mate(result[:, 9:])
    return kernel_call(
        finish_body,
        [shape(6, 3, ROWS, COLS)],
        [core_ref, mine, other],
        smem=(0,),
    )[0]


def finish_body(core, mine, other, out):
    c = core[0]
    for v in range(3):
        for l in range(3):
            out[c * 3 + v, l] = mine[:, v * 3 + l].reshape(ROWS, COLS)
            out[(1 - c) * 3 + v, l] = other[:, v * 3 + l].reshape(ROWS, COLS)


def solution(mesh):
    return jax.shard_map(
        local,
        mesh=mesh,
        in_specs=(
            P(None, "lev", "lat", "lon"),
            P(),
            P(None, "lev", None),
            P(None, "lev", None),
            P(None, "lev", ("lon", "lat")),
            P(None, "lev"),
            P(("lon", "lat")),
            P(("lon", "lat")),
        ),
        out_specs=P(None, "lev", "lat", "lon"),
        check_vma=False,
    )
```

```python
import functools

import jax
import jax.numpy as jnp
from jax import lax
from jax.experimental import pallas as pl
from jax.experimental.pallas import tpu as pltpu
from jax.sharding import PartitionSpec as P

F32, BF16, I32 = jnp.float32, jnp.bfloat16, jnp.int32
ROWS, COLS = 64, 128
TAPS = 31
STRIP = 16
LEVELS = 48
RINGS = 8
OWN = 6
SLOTS = 64
TILES = 16
OBS = 512
LON_AT, LAT_AT, WEIGHT_AT, SMALL = OBS, OBS + 128, OBS + 256, OBS + 384
PIECE = 16
VMEM = pl.BlockSpec(memory_space=pltpu.VMEM)
SMEM = pl.BlockSpec(memory_space=pltpu.SMEM)


def kernel_call(body, outs, ins, scratch=(), smem=(), flops=0, limit=16, after=()):
    moved = sum(a.size * a.dtype.itemsize for a in ins)
    moved += sum(o.size * o.dtype.itemsize for o in outs)
    count = len(after)
    return pl.pallas_call(
        lambda *refs: body(*refs[count:]),
        out_shape=list(outs),
        in_specs=[pl.BlockSpec(memory_space=pl.ANY)] * count
        + [SMEM if i in smem else VMEM for i in range(len(ins))],
        out_specs=[VMEM] * len(outs),
        scratch_shapes=list(scratch),
        compiler_params=pltpu.CompilerParams(vmem_limit_bytes=limit * 2**20),
        cost_estimate=pl.CostEstimate(flops=flops, bytes_accessed=moved, transcendentals=0),
    )(*after, *ins)


def shape(*dims, dtype=F32):
    return jax.ShapeDtypeStruct(dims, dtype)


def split(value):
    high = value.astype(BF16)
    return high, (value - high.astype(F32)).astype(BF16)


def mm(a, b):
    return jnp.dot(a, b, preferred_element_type=F32)


def mm_nt(a, b):
    return lax.dot_general(a, b, (((1,), (1,)), ((), ())), preferred_element_type=F32)


def begin_body(core, control, innovation, lon_taps, lat_taps, weight, kept, sent, kept_small, sent_small):
    c = core[0]
    kept_small[...] = jnp.zeros(kept_small.shape, F32)
    sent_small[...] = jnp.zeros(sent_small.shape, F32)
    for which, big, little in ((c, kept, kept_small), (1 - c, sent, sent_small)):
        for v in range(3):
            lon, lat, seen = [a[which * 3 + v] for a in (lon_taps, lat_taps, innovation)]
            for l in range(3):
                p = v * 3 + l
                big[p] = control[which * 3 + v, l]
                little[p, :, 0:OBS] = seen[l : l + 1]
                little[p, :, LON_AT : LON_AT + TAPS] = lon[l : l + 1]
                little[p, :, LAT_AT : LAT_AT + TAPS] = lat[l : l + 1]
                little[p, :, WEIGHT_AT:] = jnp.full((1, 128), weight[l, which * 3 + v], F32)


def arrange_body(control, mate, out):
    for p in range(9):
        out[:, p] = control[p].reshape(RINGS, 8, COLS)
        out[:, 9 + p] = mate[p].reshape(RINGS, 8, COLS)


def rows_of(v, start, count):
    return pl.ds(v * LEVELS * 8 + start, count)


def mixed(matrix, held, v, side):
    at = [pl.ds(v * LEVELS * 8 + s, LEVELS, stride=8) for s in range(8)]
    columns = jnp.concatenate([held[a, :] for a in at], axis=1)
    result = lax.dot_general(
        matrix, columns, (((side,), (0,)), ((), ())),
        precision=lax.Precision.HIGHEST, preferred_element_type=F32,
    )
    for s in range(8):
        held[at[s], :] = result[:, s * COLS : (s + 1) * COLS]


def levels_of(c, s, t, v):
    own = c if t == 0 else 1 - c
    return pl.ds(pl.multiple_of(v * LEVELS * 8 + s * 48 + own * 24, 8), 24)


def mix_body(core, got, matrix, out, held):
    c = core[0]
    for v in range(3):
        for s in range(RINGS):
            for t in range(2):
                first = t * 9 + v * 3
                held[levels_of(c, s, t, v), :] = got[s, first : first + 3].reshape(24, COLS)
        mixed(matrix[c * 3 + v], held, v, 1)
        for s in range(RINGS):
            out[s, v * OWN : (v + 1) * OWN] = held[rows_of(v, s * 48, 48), :].reshape(OWN, 8, COLS)


def unmix_body(core, got, matrix, control, out, held):
    c = core[0]
    for v in range(3):
        for s in range(RINGS):
            held[rows_of(v, s * 48, 48), :] = got[s, v * OWN : (v + 1) * OWN].reshape(48, COLS)
        mixed(matrix[c * 3 + v], held, v, 0)
        for s in range(RINGS):
            for t in range(2):
                first = t * 9 + v * 3
                part = held[levels_of(c, s, t, v), :].reshape(3, 8, COLS)
                out[s, first : first + 3] = part + control[s, first : first + 3]


def column_call(body, *ins):
    return kernel_call(
        body,
        [shape(*ins[1].shape)],
        ins,
        scratch=[pltpu.VMEM((3 * LEVELS * 8, COLS), F32)],
        smem=(0,),
        flops=2 * 3 * LEVELS * LEVELS * 1024 * 6,
    )[0]


def bands_body(core, kept, mate, high, low, back_high, back_low, lon_high, lon_low, weight):
    c = core[0]

    def toeplitz(row, height):
        full = jnp.broadcast_to(row, (height, row.shape[1]))
        return pltpu.roll(full, row.shape[1] - 15, 1, stride=1, stride_axis=0)

    def one(v, carry):
        for l in range(3):
            mine, other = kept[v * 3 + l], mate[v * 3 + l]
            for part in range(2):
                row = jnp.where(c == part, mine, other)
                p = v * OWN + part * 3 + l
                lat = toeplitz(row[:, LAT_AT : LAT_AT + 128], COLS)
                high[p], low[p] = split(lat[:ROWS])
                back_high[p], back_low[p] = split(lat.T[:ROWS])
                lon = jnp.concatenate([row[:, LON_AT : LON_AT + 128], jnp.zeros((1, 128), F32)], axis=1)
                lon_high[p], lon_low[p] = split(toeplitz(lon, COLS))
                weight[p] = row[:, WEIGHT_AT:]
        return carry

    lax.fori_loop(0, 3, one, 0)


def lat_filter(p, rows, before, after, high, low):
    extended = jnp.concatenate(
        [rows[:, p].reshape(ROWS, COLS), after, jnp.zeros((32, COLS), F32), before], axis=0
    )
    e_high, e_low = split(extended)
    return mm(high[p], e_high) + (mm(high[p], e_low) + mm(low[p], e_high))


def with_halo(l, field, left, right):
    lane = lax.broadcasted_iota(I32, (ROWS, COLS), 1)
    left = pltpu.roll(left, (COLS - STRIP - STRIP * l) % COLS, 1)
    right = pltpu.roll(right, (COLS - STRIP * l) % COLS, 1)
    halo = jnp.where(lane >= COLS - STRIP, left, jnp.where(lane < STRIP, right, 0.0))
    return split(jnp.concatenate([field, halo], axis=1))


def lon_filter(p, l, field, left, right, high, low):
    x_high, x_low = with_halo(l, field, left, right)
    return mm_nt(x_high, high[p]) + (mm_nt(x_low, high[p]) + mm_nt(x_high, low[p]))


def back_lon_filter(p, l, field, left, right, high, low):
    x_high, x_low = with_halo(l, field, left, right)
    b_high = jnp.concatenate([high[p, :, :COLS], high[p, :, COLS:]], axis=0)
    b_low = jnp.concatenate([low[p, :, :COLS], low[p, :, COLS:]], axis=0)
    return mm(x_high, b_high) + (mm(x_low, b_high) + mm(x_high, b_low))


def packed(fields):
    lane = lax.broadcasted_iota(I32, (ROWS, COLS), 1) // STRIP
    last = jnp.zeros((ROWS, COLS), F32)
    first = jnp.zeros((ROWS, COLS), F32)
    for l, field in enumerate(fields):
        last = jnp.where(lane == l, pltpu.roll(field, STRIP * (l + 1) % COLS, 1), last)
        first = jnp.where(lane == l, pltpu.roll(field, STRIP * l, 1) if l else field, first)
    return last, first


def lat_body(
    nv, latitude, rows, before, after, near, far, high, low, out, last, lead, own_rows, far_rows
):
    y = latitude[0]
    planes = nv * OWN

    def strip(at, p, there):
        both = jnp.concatenate([at[p], at[planes + p]], axis=0)
        return jnp.where(there, both, 0.0)

    def one(v, carry):
        fields = []
        for l in range(OWN):
            p = v * OWN + l
            ends = strip(before, p, y > 0), strip(after, p, y < 3)
            fields.append(lat_filter(p, rows, *ends, high, low))
        for l in range(OWN):
            out[v * OWN + l] = fields[l]
        last[v], lead[v] = packed(fields)
        return carry

    lax.fori_loop(0, nv, one, 0)
    for d, (target, block) in enumerate(((own_rows, None), (last, nv), (far_rows, None), (lead, nv))):
        first = 2 * planes + 2 * d
        came = jnp.concatenate(
            [near[d], before[first : first + 2].reshape(PIECE, COLS)]
            + [far[d], after[first : first + 2].reshape(PIECE, COLS)],
            axis=0,
        )
        if block is None:
            target[...] = came
        else:
            target[block] = came


def back_lat_body(nv, rows, before, after, high, low, out):
    def one(v, carry):
        for l in range(OWN):
            p = v * OWN + l
            ends = before[:, p].reshape(STRIP, COLS), after[:, p].reshape(STRIP, COLS)
            out[:, p] = lat_filter(p, rows, *ends, high, low).reshape(RINGS, 8, COLS)
        return carry

    lax.fori_loop(0, nv, one, 0)


def back_lon_body(nv, field, left, right, high, low, out):
    def one(v, carry):
        for l in range(OWN):
            p = v * OWN + l
            value = back_lon_filter(p, l, field[p], left[v], right[v], high, low)
            out[:, p] = value.reshape(RINGS, 8, COLS)
        return carry

    lax.fori_loop(0, nv, one, 0)


def observe_body(
    nv, field, left, right, own_rows, far_rows, high, low, weight,
    out, last, first, parts, values, misfit_high, misfit_low, row_hot, col_hot, col_hot2,
):
    arrived([own_rows[...], left[nv], far_rows[...], right[nv]], values, row_hot, col_hot, col_hot2)

    def filtered(v, carry):
        for l in range(OWN):
            p = v * OWN + l
            third = lon_filter(p, l, field[p], left[v], right[v], high, low)
            t_high, t_low = split(third)
            parts[p] = jnp.concatenate([t_high, t_low], axis=1)
        return carry

    lax.fori_loop(0, nv, filtered, 0)

    def gathered(v, carry):
        for l in range(OWN):
            p = v * OWN + l
            across = mm(parts[p], col_hot2[...])
            found = jnp.sum(across * row_hot[...], axis=0, keepdims=True)
            misfit = (found - values[p]) * jnp.concatenate([weight[p]] * 8, axis=1)
            m_high, m_low = split(misfit)
            misfit_high[p] = m_high.astype(F32)
            misfit_low[p] = m_low.astype(F32)
        return carry

    lax.fori_loop(0, nv, gathered, 0)

    def scattered(v, carry):
        fields = []
        for l in range(OWN):
            p = v * OWN + l
            w_high = (row_hot[...] * misfit_high[p]).astype(BF16)
            w_low = (row_hot[...] * misfit_low[p]).astype(BF16)
            both = mm_nt(jnp.concatenate([w_high, w_low], axis=0), col_hot[...])
            fields.append(both[:ROWS] + both[ROWS:])
            out[p] = fields[-1]
        last[v], first[v] = packed(fields)
        return carry

    lax.fori_loop(0, nv, scattered, 0)


def route_body(core, longitude, latitude, kept, mate, tile, cell, *outs):
    c = core[0]
    count = tile.shape[1]
    east = ((tile[...] >> 2) - longitude[0]) & 3
    north = ((tile[...] & 3) - latitude[0]) & 3
    away = north * 4 + east
    hot = (lax.broadcasted_iota(I32, (TILES, count), 0) == away).astype(F32)
    earlier = lax.broadcasted_iota(I32, (count, count), 0) < lax.broadcasted_iota(I32, (count, count), 1)
    before = mm(hot.astype(BF16), earlier.astype(F32).astype(BF16))
    place = jnp.sum(before * hot, axis=0, keepdims=True).astype(I32)
    slot = away * SLOTS + place
    slot_hot = (lax.broadcasted_iota(I32, (TILES * SLOTS, count), 0) == slot).astype(F32).astype(BF16)
    observed = []
    for v in range(3):
        for part in range(2):
            for l in range(3):
                p = v * 3 + l
                observed.append(jnp.where(c == part, kept[p, :, 0:OBS], mate[p, :, 0:OBS]))
    sent = jnp.concatenate(
        observed + [(cell[...] + 1).astype(F32), jnp.zeros((5, count), F32)], axis=0
    )
    high, rest = split(sent)
    remainder = sent - high.astype(F32)
    low = (remainder - rest.astype(F32)).astype(BF16)
    all_parts = mm_nt(jnp.concatenate([high, rest, low], axis=0), slot_hot)
    full = all_parts[0:24] + (all_parts[24:48] + all_parts[48:72])
    lane = lax.broadcasted_iota(I32, (8, COLS), 1)
    for e in range(TILES // 2):
        at = slice(e * COLS, (e + 1) * COLS)
        a, b, c = full[0:8, at], full[8:16, at], full[16:24, at]
        a2, b2, c2 = [pltpu.roll(x, SLOTS, 1) for x in (a, b, c)]
        out, d = outs[e // 2], e % 2 * 2
        out[d, 0:8] = jnp.where(lane < SLOTS, a, b2)
        out[d, 8:16] = jnp.where(lane < SLOTS, c, 0.0)
        out[d + 1, 0:8] = jnp.where(lane < SLOTS, a2, b)
        out[d + 1, 8:16] = jnp.where(lane < SLOTS, c2, 0.0)


def arrived(blocks, values, row_hot, col_hot, col_hot2):
    low = lax.broadcasted_iota(I32, (8, COLS), 1) < SLOTS
    full = []
    for block in blocks:
        for first in (0, 2 * PIECE):
            a, c, b, d = [block[first + 8 * i : first + 8 * i + 8] for i in range(4)]
            full.append(
                jnp.concatenate(
                    [
                        jnp.where(low, a, pltpu.roll(b, SLOTS, 1)),
                        jnp.where(low, pltpu.roll(a, SLOTS, 1), b),
                        jnp.where(low, c, pltpu.roll(d, SLOTS, 1)),
                    ],
                    axis=0,
                )
            )
    full = jnp.concatenate(full, axis=1)
    for p in range(18):
        values[p] = full[p : p + 1]
    cell = full[18:19].astype(I32) - 1
    count = cell.shape[1]
    row_hot[...] = (lax.broadcasted_iota(I32, (ROWS, count), 0) == (cell >> 7)).astype(F32)
    cols = (lax.broadcasted_iota(I32, (COLS, count), 0) == (cell & 127)).astype(F32).astype(BF16)
    col_hot[...] = cols
    col_hot2[0:COLS] = cols
    col_hot2[COLS : 2 * COLS] = cols


def neighbours(axis, wrap):
    size = lax.axis_size(axis)
    up = [(i, (i + 1) % size) for i in range(size if wrap else size - 1)]
    return up, [(j, i) for i, j in up]


def exchanged(last, first, axis, wrap):
    up, down = neighbours(axis, wrap)
    return lax.ppermute(last, axis, up), lax.ppermute(first, axis, down)


def across(value, axis):
    size = lax.axis_size(axis)
    return lax.ppermute(value, axis, [(i, (i + 2) % size) for i in range(size)])


def with_mate(value):
    pairs = [(i, i ^ 1) for i in range(lax.axis_size("lev"))]
    return lax.ppermute(value, "lev", pairs)


def over_rings(value):
    size = lax.axis_size("lev")
    groups = [list(range(0, size, 2)), list(range(1, size, 2))]
    return lax.all_to_all(value, "lev", 0, 0, tiled=True, axis_index_groups=groups)


def local(control, vertical, lon_taps, lat_taps, innovation, inv_variance, obs_tile, obs_cell):
    def index(axis):
        return lax.axis_index(axis).astype(I32).reshape(1)

    core, longitude, latitude = index("lev") % 2, index("lon"), index("lat")
    nv = 3
    planes = nv * OWN
    slots = TILES * SLOTS

    block, small_block = shape(9, ROWS, COLS), shape(9, 1, SMALL)
    kept, sent, kept_small, sent_small = kernel_call(
        begin_body,
        [block, block, small_block, small_block],
        [core, control, innovation, lon_taps, lat_taps, jnp.swapaxes(inv_variance, 0, 1)],
        smem=(0, 5),
    )
    mate_small = with_mate(sent_small)
    mate_control = with_mate(sent)
    piece = shape(4, PIECE, COLS)
    near, north, far, south = kernel_call(
        route_body,
        [piece] * 4,
        [core, longitude, latitude, kept_small, mate_small, obs_tile.reshape(1, -1), obs_cell.reshape(1, -1)],
        smem=(0, 1, 2),
        flops=2 * 72 * slots * obs_tile.shape[0],
    )
    arranged = kernel_call(
        arrange_body,
        [shape(RINGS, planes, 8, COLS)],
        [kept, mate_control],
        after=(near,),
    )[0]
    columns = over_rings(arranged)
    first = over_rings(column_call(mix_body, core, columns, vertical))

    def with_rows(strips, rows):
        return jnp.concatenate([strips.reshape(-1, 8, COLS), rows.reshape(-1, 8, COLS)], axis=0)

    before, after = exchanged(with_rows(first[6:8], north), with_rows(first[0:2], south), "lat", True)
    far = across(far, "lat")
    high, low, back_high, back_low, lon_high, lon_low, weight = kernel_call(
        bands_body,
        [shape(planes, ROWS, 128, dtype=BF16)] * 4
        + [shape(planes, COLS, 256, dtype=BF16)] * 2
        + [shape(planes, 1, 128)],
        [core, kept_small, mate_small],
        smem=(0,),
        flops=planes * 200000,
        after=(first,),
    )
    field_shape = shape(planes, ROWS, COLS)
    lat_flops = 2 * 3 * planes * ROWS * 128 * COLS
    row_block = shape(4 * PIECE, COLS)
    field, last, lead, own_rows, far_rows = kernel_call(
        functools.partial(lat_body, nv),
        [field_shape] + [shape(nv + 1, ROWS, COLS)] * 2 + [row_block] * 2,
        [latitude, first, before, after, near, far, high, low],
        smem=(0,),
        flops=lat_flops,
    )
    left, right = exchanged(last, lead, "lon", True)
    far_rows = across(far_rows, "lon")
    pack_shape = shape(nv, ROWS, COLS)
    placed, last, lead = kernel_call(
        functools.partial(observe_body, nv),
        [field_shape, pack_shape, pack_shape],
        [field, left, right, own_rows, far_rows, lon_high, lon_low, weight],
        scratch=[
            pltpu.VMEM((planes, ROWS, 2 * COLS), BF16),
            pltpu.VMEM((planes, 1, slots), F32),
            pltpu.VMEM((planes, 1, slots), F32),
            pltpu.VMEM((planes, 1, slots), F32),
            pltpu.VMEM((ROWS, slots), F32),
            pltpu.VMEM((COLS, slots), BF16),
            pltpu.VMEM((2 * COLS, slots), BF16),
        ],
        flops=2 * planes * ROWS * slots * 256 * 2,
    )
    left, right = exchanged(last, lead, "lon", True)
    back = kernel_call(
        functools.partial(back_lon_body, nv),
        [shape(RINGS, planes, 8, COLS)],
        [placed, left, right, lon_high, lon_low],
        flops=2 * lat_flops,
    )[0]
    before, after = exchanged(back[6:8], back[0:2], "lat", False)
    back = kernel_call(
        functools.partial(back_lat_body, nv),
        [shape(RINGS, planes, 8, COLS)],
        [back, before, after, back_high, back_low],
        flops=lat_flops,
    )[0]
    result = over_rings(column_call(unmix_body, core, over_rings(back), vertical, columns))

    mine, other = result[:, :9], with_mate(result[:, 9:])
    return kernel_call(
        finish_body,
        [shape(6, 3, ROWS, COLS)],
        [core, mine, other],
        smem=(0,),
    )[0]


def finish_body(core, mine, other, out):
    c = core[0]
    for v in range(3):
        for l in range(3):
            out[c * 3 + v, l] = mine[:, v * 3 + l].reshape(ROWS, COLS)
            out[(1 - c) * 3 + v, l] = other[:, v * 3 + l].reshape(ROWS, COLS)


def solution(mesh):
    return jax.shard_map(
        local,
        mesh=mesh,
        in_specs=(
            P(None, "lev", "lat", "lon"),
            P(),
            P(None, "lev", None),
            P(None, "lev", None),
            P(None, "lev", ("lon", "lat")),
            P(None, "lev"),
            P(("lon", "lat")),
            P(("lon", "lat")),
        ),
        out_specs=P(None, "lev", "lat", "lon"),
        check_vma=False,
    )
```

```python
import functools

import jax
import jax.numpy as jnp
from jax import lax
from jax.experimental import pallas as pl
from jax.experimental.pallas import tpu as pltpu
from jax.sharding import PartitionSpec as P

F32, BF16, I32 = jnp.float32, jnp.bfloat16, jnp.int32
ROWS, COLS = 64, 128
TAPS = 31
STRIP = 16
LEVELS = 48
RINGS = 8
OWN = 6
SLOTS = 64
TILES = 16
OBS = 512
LON_AT, LAT_AT, WEIGHT_AT, SMALL = OBS, OBS + 128, OBS + 256, OBS + 384
PIECE = 16
VMEM = pl.BlockSpec(memory_space=pltpu.VMEM)
SMEM = pl.BlockSpec(memory_space=pltpu.SMEM)


def kernel_call(body, outs, ins, scratch=(), smem=(), flops=0, limit=16, after=()):
    moved = sum(a.size * a.dtype.itemsize for a in ins)
    moved += sum(o.size * o.dtype.itemsize for o in outs)
    count = len(after)
    return pl.pallas_call(
        lambda *refs: body(*refs[count:]),
        out_shape=list(outs),
        in_specs=[pl.BlockSpec(memory_space=pl.ANY)] * count
        + [SMEM if i in smem else VMEM for i in range(len(ins))],
        out_specs=[VMEM] * len(outs),
        scratch_shapes=list(scratch),
        compiler_params=pltpu.CompilerParams(vmem_limit_bytes=limit * 2**20),
        cost_estimate=pl.CostEstimate(flops=flops, bytes_accessed=moved, transcendentals=0),
    )(*after, *ins)


def shape(*dims, dtype=F32):
    return jax.ShapeDtypeStruct(dims, dtype)


def split(value):
    high = value.astype(BF16)
    return high, (value - high.astype(F32)).astype(BF16)


def mm(a, b):
    return jnp.dot(a, b, preferred_element_type=F32)


def mm_nt(a, b):
    return lax.dot_general(a, b, (((1,), (1,)), ((), ())), preferred_element_type=F32)


def begin_body(core, control, kept, sent):
    c = core[0]
    for which, big in ((c, kept), (1 - c, sent)):
        for v in range(3):
            for l in range(3):
                big[v * 3 + l] = control[which * 3 + v, l]


def small_body(core, innovation, lon_taps, lat_taps, weight, kept, sent):
    c = core[0]
    kept[...] = jnp.zeros(kept.shape, F32)
    sent[...] = jnp.zeros(sent.shape, F32)
    for which, little in ((c, kept), (1 - c, sent)):
        for v in range(3):
            lon, lat, seen = [a[which * 3 + v] for a in (lon_taps, lat_taps, innovation)]
            for l in range(3):
                p = v * 3 + l
                little[p, :, 0:OBS] = seen[l : l + 1]
                little[p, :, LON_AT : LON_AT + TAPS] = lon[l : l + 1]
                little[p, :, LAT_AT : LAT_AT + TAPS] = lat[l : l + 1]
                little[p, :, WEIGHT_AT:] = jnp.full((1, 128), weight[l, which * 3 + v], F32)


def arrange_body(control, mate, out):
    for p in range(9):
        out[:, p] = control[p].reshape(RINGS, 8, COLS)
        out[:, 9 + p] = mate[p].reshape(RINGS, 8, COLS)


def rows_of(v, start, count):
    return pl.ds(v * LEVELS * 8 + start, count)


def mixed(matrix, held, v, side):
    at = [pl.ds(v * LEVELS * 8 + s, LEVELS, stride=8) for s in range(8)]
    columns = jnp.concatenate([held[a, :] for a in at], axis=1)
    result = lax.dot_general(
        matrix, columns, (((side,), (0,)), ((), ())),
        precision=lax.Precision.HIGHEST, preferred_element_type=F32,
    )
    for s in range(8):
        held[at[s], :] = result[:, s * COLS : (s + 1) * COLS]


def levels_of(c, s, t, v):
    own = c if t == 0 else 1 - c
    return pl.ds(pl.multiple_of(v * LEVELS * 8 + s * 48 + own * 24, 8), 24)


def mix_body(core, got, matrix, out, held):
    c = core[0]
    for v in range(3):
        for s in range(RINGS):
            for t in range(2):
                first = t * 9 + v * 3
                held[levels_of(c, s, t, v), :] = got[s, first : first + 3].reshape(24, COLS)
        mixed(matrix[c * 3 + v], held, v, 1)
        for s in range(RINGS):
            out[s, v * OWN : (v + 1) * OWN] = held[rows_of(v, s * 48, 48), :].reshape(OWN, 8, COLS)


def unmix_body(core, got, matrix, control, out, held):
    c = core[0]
    for v in range(3):
        for s in range(RINGS):
            held[rows_of(v, s * 48, 48), :] = got[s, v * OWN : (v + 1) * OWN].reshape(48, COLS)
        mixed(matrix[c * 3 + v], held, v, 0)
        for s in range(RINGS):
            for t in range(2):
                first = t * 9 + v * 3
                part = held[levels_of(c, s, t, v), :].reshape(3, 8, COLS)
                out[s, first : first + 3] = part + control[s, first : first + 3]


def column_call(body, *ins, after=()):
    return kernel_call(
        body,
        [shape(*ins[1].shape)],
        ins,
        scratch=[pltpu.VMEM((3 * LEVELS * 8, COLS), F32)],
        smem=(0,),
        flops=2 * 3 * LEVELS * LEVELS * 1024 * 6,
        after=after,
    )[0]


def bands_body(core, kept, mate, high, low, back_high, back_low, lon_high, lon_low, weight):
    c = core[0]

    def toeplitz(row, height):
        full = jnp.broadcast_to(row, (height, row.shape[1]))
        return pltpu.roll(full, row.shape[1] - 15, 1, stride=1, stride_axis=0)

    def one(v, carry):
        for l in range(3):
            mine, other = kept[v * 3 + l], mate[v * 3 + l]
            for part in range(2):
                row = jnp.where(c == part, mine, other)
                p = v * OWN + part * 3 + l
                lat = toeplitz(row[:, LAT_AT : LAT_AT + 128], COLS)
                high[p], low[p] = split(lat[:ROWS])
                back_high[p], back_low[p] = split(lat.T[:ROWS])
                lon = jnp.concatenate([row[:, LON_AT : LON_AT + 128], jnp.zeros((1, 128), F32)], axis=1)
                lon_high[p], lon_low[p] = split(toeplitz(lon, COLS))
                weight[p] = row[:, WEIGHT_AT:]
        return carry

    lax.fori_loop(0, 3, one, 0)


def lat_filter(p, rows, before, after, high, low):
    extended = jnp.concatenate(
        [rows[:, p].reshape(ROWS, COLS), after, jnp.zeros((32, COLS), F32), before], axis=0
    )
    e_high, e_low = split(extended)
    return mm(high[p], e_high) + (mm(high[p], e_low) + mm(low[p], e_high))


def with_halo(l, field, left, right):
    lane = lax.broadcasted_iota(I32, (ROWS, COLS), 1)
    left = pltpu.roll(left, (COLS - STRIP - STRIP * l) % COLS, 1)
    right = pltpu.roll(right, (COLS - STRIP * l) % COLS, 1)
    halo = jnp.where(lane >= COLS - STRIP, left, jnp.where(lane < STRIP, right, 0.0))
    return split(jnp.concatenate([field, halo], axis=1))


def lon_filter(p, l, field, left, right, high, low):
    x_high, x_low = with_halo(l, field, left, right)
    return mm_nt(x_high, high[p]) + (mm_nt(x_low, high[p]) + mm_nt(x_high, low[p]))


def back_lon_filter(p, l, field, left, right, high, low):
    x_high, x_low = with_halo(l, field, left, right)
    b_high = jnp.concatenate([high[p, :, :COLS], high[p, :, COLS:]], axis=0)
    b_low = jnp.concatenate([low[p, :, :COLS], low[p, :, COLS:]], axis=0)
    return mm(x_high, b_high) + (mm(x_low, b_high) + mm(x_high, b_low))


def packed(fields):
    lane = lax.broadcasted_iota(I32, (ROWS, COLS), 1) // STRIP
    last = jnp.zeros((ROWS, COLS), F32)
    first = jnp.zeros((ROWS, COLS), F32)
    for l, field in enumerate(fields):
        last = jnp.where(lane == l, pltpu.roll(field, STRIP * (l + 1) % COLS, 1), last)
        first = jnp.where(lane == l, pltpu.roll(field, STRIP * l, 1) if l else field, first)
    return last, first


def lat_body(
    nv, latitude, rows, before, after, near, far, high, low, out, last, lead, own_rows, far_rows
):
    y = latitude[0]
    planes = nv * OWN

    def strip(at, p, there):
        both = jnp.concatenate([at[p], at[planes + p]], axis=0)
        return jnp.where(there, both, 0.0)

    def one(v, carry):
        fields = []
        for l in range(OWN):
            p = v * OWN + l
            ends = strip(before, p, y > 0), strip(after, p, y < 3)
            fields.append(lat_filter(p, rows, *ends, high, low))
        for l in range(OWN):
            out[v * OWN + l] = fields[l]
        last[v], lead[v] = packed(fields)
        return carry

    lax.fori_loop(0, nv, one, 0)
    for d, (target, block) in enumerate(((own_rows, None), (last, nv), (lead, nv), (far_rows, None))):
        first = 2 * planes + 2 * d
        came = jnp.concatenate(
            [near[d], before[first : first + 2].reshape(PIECE, COLS)]
            + [far[d], after[first : first + 2].reshape(PIECE, COLS)],
            axis=0,
        )
        if block is None:
            target[...] = came
        else:
            target[block] = came


def back_lat_body(nv, latitude, rows, before, after, high, low, out):
    y = latitude[0]

    def one(v, carry):
        for l in range(OWN):
            p = v * OWN + l
            ends = (
                jnp.where(y > 0, before[:, p].reshape(STRIP, COLS), 0.0),
                jnp.where(y < 3, after[:, p].reshape(STRIP, COLS), 0.0),
            )
            out[:, p] = lat_filter(p, rows, *ends, high, low).reshape(RINGS, 8, COLS)
        return carry

    lax.fori_loop(0, nv, one, 0)


def back_lon_body(nv, field, left, right, high, low, out):
    def one(v, carry):
        for l in range(OWN):
            p = v * OWN + l
            value = back_lon_filter(p, l, field[p], left[v], right[v], high, low)
            out[:, p] = value.reshape(RINGS, 8, COLS)
        return carry

    lax.fori_loop(0, nv, one, 0)


def observe_body(
    nv, field, left, right, own_rows, far_rows, high, low, weight,
    out, last, first, parts, values, misfit_high, misfit_low, row_hot, col_hot, col_hot2,
):
    arrived([own_rows[...], left[nv], far_rows[...], right[nv]], values, row_hot, col_hot, col_hot2)

    def filtered(v, carry):
        for l in range(OWN):
            p = v * OWN + l
            third = lon_filter(p, l, field[p], left[v], right[v], high, low)
            t_high, t_low = split(third)
            parts[p] = jnp.concatenate([t_high, t_low], axis=1)
        return carry

    lax.fori_loop(0, nv, filtered, 0)

    def gathered(v, carry):
        block = parts[pl.ds(v * OWN, OWN)].reshape(OWN * ROWS, 2 * COLS)
        across = mm(block, col_hot2[...])
        for l in range(OWN):
            p = v * OWN + l
            found = jnp.sum(across[l * ROWS : (l + 1) * ROWS] * row_hot[...], axis=0, keepdims=True)
            misfit = (found - values[p]) * jnp.concatenate([weight[p]] * 8, axis=1)
            m_high, m_low = split(misfit)
            misfit_high[p] = m_high.astype(F32)
            misfit_low[p] = m_low.astype(F32)
        return carry

    lax.fori_loop(0, nv, gathered, 0)

    def scattered(v, carry):
        placed = []
        for l in range(OWN):
            p = v * OWN + l
            placed.append((row_hot[...] * misfit_high[p]).astype(BF16))
            placed.append((row_hot[...] * misfit_low[p]).astype(BF16))
        both = mm_nt(jnp.concatenate(placed, axis=0), col_hot[...])
        fields = []
        for l in range(OWN):
            at = 2 * l * ROWS
            fields.append(both[at : at + ROWS] + both[at + ROWS : at + 2 * ROWS])
            out[v * OWN + l] = fields[-1]
        last[v], first[v] = packed(fields)
        return carry

    lax.fori_loop(0, nv, scattered, 0)


def route_body(core, longitude, latitude, kept, mate, tile, cell, out, half_way):
    c = core[0]
    count = tile.shape[1]
    east = ((tile[...] >> 2) - longitude[0]) & 3
    north = ((tile[...] & 3) - latitude[0]) & 3
    away = north * 4 + east
    hot = (lax.broadcasted_iota(I32, (TILES, count), 0) == away).astype(F32)
    earlier = lax.broadcasted_iota(I32, (count, count), 0) < lax.broadcasted_iota(I32, (count, count), 1)
    before = mm(hot.astype(BF16), earlier.astype(F32).astype(BF16))
    place = jnp.sum(before * hot, axis=0, keepdims=True).astype(I32)
    slot = away * SLOTS + place
    slot_hot = (lax.broadcasted_iota(I32, (TILES * SLOTS, count), 0) == slot).astype(F32).astype(BF16)
    observed = []
    for v in range(3):
        for part in range(2):
            for l in range(3):
                p = v * 3 + l
                observed.append(jnp.where(c == part, kept[p, :, 0:OBS], mate[p, :, 0:OBS]))
    sent = jnp.concatenate(
        observed + [(cell[...] + 1).astype(F32), jnp.zeros((5, count), F32)], axis=0
    )
    high, rest = split(sent)
    remainder = sent - high.astype(F32)
    low = (remainder - rest.astype(F32)).astype(BF16)
    all_parts = mm_nt(jnp.concatenate([high, rest, low], axis=0), slot_hot)
    full = all_parts[0:24] + (all_parts[24:48] + all_parts[48:72])
    lane = lax.broadcasted_iota(I32, (8, COLS), 1)
    for e in range(TILES // 2):
        at = slice(e * COLS, (e + 1) * COLS)
        a, b, c = full[0:8, at], full[8:16, at], full[16:24, at]
        a2, b2, c2 = [pltpu.roll(x, SLOTS, 1) for x in (a, b, c)]
        pair = (
            (jnp.where(lane < SLOTS, a, b2), jnp.where(lane < SLOTS, c, 0.0)),
            (jnp.where(lane < SLOTS, a2, b), jnp.where(lane < SLOTS, c2, 0.0)),
        )
        for i in range(2):
            target, at = (out, (e // 2, i)) if e % 2 == 0 else ((half_way, (e // 2,)), (out, (e // 2, 2)))[i]
            target[(*at, slice(0, 8))], target[(*at, slice(8, 16))] = pair[i]


def arrived(blocks, values, row_hot, col_hot, col_hot2):
    low = lax.broadcasted_iota(I32, (8, COLS), 1) < SLOTS
    full = []
    for block in blocks:
        for first in (0, 2 * PIECE):
            a, c, b, d = [block[first + 8 * i : first + 8 * i + 8] for i in range(4)]
            full.append(
                jnp.concatenate(
                    [
                        jnp.where(low, a, pltpu.roll(b, SLOTS, 1)),
                        jnp.where(low, pltpu.roll(a, SLOTS, 1), b),
                        jnp.where(low, c, pltpu.roll(d, SLOTS, 1)),
                    ],
                    axis=0,
                )
            )
    full = jnp.concatenate(full, axis=1)
    for p in range(18):
        values[p] = full[p : p + 1]
    cell = full[18:19].astype(I32) - 1
    count = cell.shape[1]
    row_hot[...] = (lax.broadcasted_iota(I32, (ROWS, count), 0) == (cell >> 7)).astype(F32)
    cols = (lax.broadcasted_iota(I32, (COLS, count), 0) == (cell & 127)).astype(F32).astype(BF16)
    col_hot[...] = cols
    col_hot2[0:COLS] = cols
    col_hot2[COLS : 2 * COLS] = cols


def exchanged(last, first, axis):
    size = lax.axis_size(axis)
    up = [(i, (i + 1) % size) for i in range(size)]
    down = [(j, i) for i, j in up]
    return lax.ppermute(last, axis, up), lax.ppermute(first, axis, down)


def across(value, axis):
    size = lax.axis_size(axis)
    return lax.ppermute(value, axis, [(i, (i + 2) % size) for i in range(size)])


def with_mate(value):
    pairs = [(i, i ^ 1) for i in range(lax.axis_size("lev"))]
    return lax.ppermute(value, "lev", pairs)


def over_rings(value):
    size = lax.axis_size("lev")
    groups = [list(range(0, size, 2)), list(range(1, size, 2))]
    return lax.all_to_all(value, "lev", 0, 0, tiled=True, axis_index_groups=groups)


def local(control, vertical, lon_taps, lat_taps, innovation, inv_variance, obs_tile, obs_cell):
    def index(axis):
        return lax.axis_index(axis).astype(I32).reshape(1)

    core, longitude, latitude = index("lev") % 2, index("lon"), index("lat")
    nv = 3
    planes = nv * OWN
    slots = TILES * SLOTS

    block, small_block = shape(9, ROWS, COLS), shape(9, 1, SMALL)
    kept, sent = kernel_call(begin_body, [block, block], [core, control], smem=(0,))
    arranged = kernel_call(
        arrange_body, [shape(RINGS, planes, 8, COLS)], [kept, with_mate(sent)]
    )[0]
    columns = over_rings(arranged)

    kept_small, sent_small = kernel_call(
        small_body,
        [small_block, small_block],
        [core, innovation, lon_taps, lat_taps, jnp.swapaxes(inv_variance, 0, 1)],
        smem=(0, 4),
        after=(arranged,),
    )
    mate_small = with_mate(sent_small)
    routed, half_way = kernel_call(
        route_body,
        [shape(4, 3, PIECE, COLS), shape(4, PIECE, COLS)],
        [core, longitude, latitude, kept_small, mate_small, obs_tile.reshape(1, -1), obs_cell.reshape(1, -1)],
        smem=(0, 1, 2),
        flops=2 * 72 * slots * obs_tile.shape[0],
    )
    pieces = jnp.concatenate([routed, across(half_way, "lon")[:, None]], axis=1)
    far = across(pieces[2], "lat")
    high, low, back_high, back_low, lon_high, lon_low, weight = kernel_call(
        bands_body,
        [shape(planes, ROWS, 128, dtype=BF16)] * 4
        + [shape(planes, COLS, 256, dtype=BF16)] * 2
        + [shape(planes, 1, 128)],
        [core, kept_small, mate_small],
        smem=(0,),
        flops=planes * 200000,
    )
    first = over_rings(column_call(mix_body, core, columns, vertical, after=(far, weight)))

    def with_rows(strips, rows):
        return jnp.concatenate([strips.reshape(-1, 8, COLS), rows.reshape(-1, 8, COLS)], axis=0)

    before, after = exchanged(
        with_rows(first[6:8], pieces[1]), with_rows(first[0:2], pieces[3]), "lat"
    )
    field_shape = shape(planes, ROWS, COLS)
    lat_flops = 2 * 3 * planes * ROWS * 128 * COLS
    row_block = shape(4 * PIECE, COLS)
    field, last, lead, own_rows, far_rows = kernel_call(
        functools.partial(lat_body, nv),
        [field_shape] + [shape(nv + 1, ROWS, COLS)] * 2 + [row_block] * 2,
        [latitude, first, before, after, pieces[0], far, high, low],
        smem=(0,),
        flops=lat_flops,
    )
    left, right = exchanged(last, lead, "lon")
    pack_shape = shape(nv, ROWS, COLS)
    placed, last, lead = kernel_call(
        functools.partial(observe_body, nv),
        [field_shape, pack_shape, pack_shape],
        [field, left, right, own_rows, far_rows, lon_high, lon_low, weight],
        scratch=[
            pltpu.VMEM((planes, ROWS, 2 * COLS), BF16),
            pltpu.VMEM((planes, 1, slots), F32),
            pltpu.VMEM((planes, 1, slots), F32),
            pltpu.VMEM((planes, 1, slots), F32),
            pltpu.VMEM((ROWS, slots), F32),
            pltpu.VMEM((COLS, slots), BF16),
            pltpu.VMEM((2 * COLS, slots), BF16),
        ],
        flops=2 * planes * ROWS * slots * 256 * 2,
    )
    left, right = exchanged(last, lead, "lon")
    back = kernel_call(
        functools.partial(back_lon_body, nv),
        [shape(RINGS, planes, 8, COLS)],
        [placed, left, right, lon_high, lon_low],
        flops=2 * lat_flops,
    )[0]
    before, after = exchanged(back[6:8], back[0:2], "lat")
    back = kernel_call(
        functools.partial(back_lat_body, nv),
        [shape(RINGS, planes, 8, COLS)],
        [latitude, back, before, after, back_high, back_low],
        smem=(0,),
        flops=lat_flops,
    )[0]
    result = over_rings(column_call(unmix_body, core, over_rings(back), vertical, columns))

    mine, other = result[:, :9], with_mate(result[:, 9:])
    return kernel_call(
        finish_body,
        [shape(6, 3, ROWS, COLS)],
        [core, mine, other],
        smem=(0,),
    )[0]


def finish_body(core, mine, other, out):
    c = core[0]
    for v in range(3):
        for l in range(3):
            out[c * 3 + v, l] = mine[:, v * 3 + l].reshape(ROWS, COLS)
            out[(1 - c) * 3 + v, l] = other[:, v * 3 + l].reshape(ROWS, COLS)


def solution(mesh):
    return jax.shard_map(
        local,
        mesh=mesh,
        in_specs=(
            P(None, "lev", "lat", "lon"),
            P(),
            P(None, "lev", None),
            P(None, "lev", None),
            P(None, "lev", ("lon", "lat")),
            P(None, "lev"),
            P(("lon", "lat")),
            P(("lon", "lat")),
        ),
        out_specs=P(None, "lev", "lat", "lon"),
        check_vma=False,
    )
```

```python
import functools

import jax
import jax.numpy as jnp
from jax import lax
from jax.experimental import pallas as pl
from jax.experimental.pallas import tpu as pltpu
from jax.sharding import PartitionSpec as P

F32, BF16, I32 = jnp.float32, jnp.bfloat16, jnp.int32
ROWS, COLS = 64, 128
TAPS = 31
STRIP = 16
LEVELS = 48
RINGS = 8
OWN = 6
SLOTS = 64
TILES = 16
OBS = 512
LON_AT, LAT_AT, WEIGHT_AT, SMALL = OBS, OBS + 128, OBS + 256, OBS + 384
PIECE = 16
VMEM = pl.BlockSpec(memory_space=pltpu.VMEM)
SMEM = pl.BlockSpec(memory_space=pltpu.SMEM)


def kernel_call(body, outs, ins, scratch=(), smem=(), flops=0, limit=16, after=()):
    moved = sum(a.size * a.dtype.itemsize for a in ins)
    moved += sum(o.size * o.dtype.itemsize for o in outs)
    count = len(after)
    return pl.pallas_call(
        lambda *refs: body(*refs[count:]),
        out_shape=list(outs),
        in_specs=[pl.BlockSpec(memory_space=pl.ANY)] * count
        + [SMEM if i in smem else VMEM for i in range(len(ins))],
        out_specs=[VMEM] * len(outs),
        scratch_shapes=list(scratch),
        compiler_params=pltpu.CompilerParams(vmem_limit_bytes=limit * 2**20),
        cost_estimate=pl.CostEstimate(flops=flops, bytes_accessed=moved, transcendentals=0),
    )(*after, *ins)


def shape(*dims, dtype=F32):
    return jax.ShapeDtypeStruct(dims, dtype)


def split(value):
    high = value.astype(BF16)
    return high, (value - high.astype(F32)).astype(BF16)


def mm(a, b):
    return jnp.dot(a, b, preferred_element_type=F32)


def mm_nt(a, b):
    return lax.dot_general(a, b, (((1,), (1,)), ((), ())), preferred_element_type=F32)


def begin_body(core, control, kept, sent):
    c = core[0]
    for which, big in ((c, kept), (1 - c, sent)):
        for v in range(3):
            for l in range(3):
                big[v * 3 + l] = control[which * 3 + v, l]


def small_body(core, innovation, lon_taps, lat_taps, weight, kept, sent):
    c = core[0]
    kept[...] = jnp.zeros(kept.shape, F32)
    sent[...] = jnp.zeros(sent.shape, F32)
    for which, little in ((c, kept), (1 - c, sent)):
        for v in range(3):
            lon, lat, seen = [a[which * 3 + v] for a in (lon_taps, lat_taps, innovation)]
            for l in range(3):
                p = v * 3 + l
                little[p, :, 0:OBS] = seen[l : l + 1]
                little[p, :, LON_AT : LON_AT + TAPS] = lon[l : l + 1]
                little[p, :, LAT_AT : LAT_AT + TAPS] = lat[l : l + 1]
                little[p, :, WEIGHT_AT:] = jnp.full((1, 128), weight[l, which * 3 + v], F32)


def arrange_body(control, mate, out):
    for p in range(9):
        out[:, p] = control[p].reshape(RINGS, 8, COLS)
        out[:, 9 + p] = mate[p].reshape(RINGS, 8, COLS)


def rows_of(v, start, count):
    return pl.ds(v * LEVELS * 8 + start, count)


def mixed(matrix, held, v, side):
    at = [pl.ds(v * LEVELS * 8 + s, LEVELS, stride=8) for s in range(8)]
    columns = jnp.concatenate([held[a, :] for a in at], axis=1)
    result = lax.dot_general(
        matrix, columns, (((side,), (0,)), ((), ())),
        precision=lax.Precision.HIGHEST, preferred_element_type=F32,
    )
    for s in range(8):
        held[at[s], :] = result[:, s * COLS : (s + 1) * COLS]


def chip_order(c, part, own, mate):
    return jnp.where(c == part, own, mate)


def mix_body(core, got, matrix, out, held):
    c = core[0]
    for v in range(3):
        for s in range(RINGS):
            own, mate = got[s, v * 3 : v * 3 + 3], got[s, 9 + v * 3 : 12 + v * 3]
            for part in range(2):
                value = chip_order(c, part, own, mate)
                held[rows_of(v, s * 48 + part * 24, 24), :] = value.reshape(24, COLS)
        mixed(matrix[c * 3 + v], held, v, 1)
        for s in range(RINGS):
            out[s, v * OWN : (v + 1) * OWN] = held[rows_of(v, s * 48, 48), :].reshape(OWN, 8, COLS)


def unmix_body(core, got, matrix, control, out, held):
    c = core[0]
    for v in range(3):
        for s in range(RINGS):
            held[rows_of(v, s * 48, 48), :] = got[s, v * OWN : (v + 1) * OWN].reshape(48, COLS)
        mixed(matrix[c * 3 + v], held, v, 0)
        for s in range(RINGS):
            lower, upper = [held[rows_of(v, s * 48 + h * 24, 24), :].reshape(3, 8, COLS) for h in range(2)]
            for t in range(2):
                first = t * 9 + v * 3
                part = chip_order(c, t, lower, upper)
                out[s, first : first + 3] = part + control[s, first : first + 3]


def column_call(body, *ins, after=()):
    return kernel_call(
        body,
        [shape(*ins[1].shape)],
        ins,
        scratch=[pltpu.VMEM((3 * LEVELS * 8, COLS), F32)],
        smem=(0,),
        flops=2 * 3 * LEVELS * LEVELS * 1024 * 6,
        after=after,
    )[0]


def bands_body(core, kept, mate, high, low, back_high, back_low, lon_high, lon_low, weight):
    c = core[0]

    def toeplitz(row, height):
        full = jnp.broadcast_to(row, (height, row.shape[1]))
        return pltpu.roll(full, row.shape[1] - 15, 1, stride=1, stride_axis=0)

    def one(v, carry):
        for l in range(3):
            mine, other = kept[v * 3 + l], mate[v * 3 + l]
            for part in range(2):
                row = jnp.where(c == part, mine, other)
                p = v * OWN + part * 3 + l
                lat = toeplitz(row[:, LAT_AT : LAT_AT + 128], COLS)
                high[p], low[p] = split(lat[:ROWS])
                back_high[p], back_low[p] = split(lat.T[:ROWS])
                lon = jnp.concatenate([row[:, LON_AT : LON_AT + 128], jnp.zeros((1, 128), F32)], axis=1)
                lon_high[p], lon_low[p] = split(toeplitz(lon, COLS))
                weight[p] = row[:, WEIGHT_AT:]
        return carry

    lax.fori_loop(0, 3, one, 0)


def lat_filter(p, rows, before, after, high, low):
    extended = jnp.concatenate(
        [rows[:, p].reshape(ROWS, COLS), after, jnp.zeros((32, COLS), F32), before], axis=0
    )
    e_high, e_low = split(extended)
    return mm(high[p], e_high) + (mm(high[p], e_low) + mm(low[p], e_high))


PACKED = 48


def unpacked(pack, l, base):
    block = pack[l // 2 * STRIP : (l // 2 + 1) * STRIP]
    return jnp.concatenate(
        [
            pltpu.roll(pack, (base - STRIP * l) % COLS, 1) if (base - STRIP * l) % COLS else pack,
            pltpu.roll(block, (base - STRIP * (OWN + l % 2)) % COLS, 1),
        ],
        axis=0,
    )


def with_halo(l, field, left, right):
    lane = lax.broadcasted_iota(I32, (ROWS, COLS), 1)
    left, right = unpacked(left, l, COLS - STRIP), unpacked(right, l, 0)
    halo = jnp.where(lane >= COLS - STRIP, left, jnp.where(lane < STRIP, right, 0.0))
    return split(jnp.concatenate([field, halo], axis=1))


def lon_filter(p, l, field, left, right, high, low):
    x_high, x_low = with_halo(l, field, left, right)
    return mm_nt(x_high, high[p]) + (mm_nt(x_low, high[p]) + mm_nt(x_high, low[p]))


def back_lon_filter(p, l, field, left, right, high, low):
    x_high, x_low = with_halo(l, field, left, right)
    b_high = jnp.concatenate([high[p, :, :COLS], high[p, :, COLS:]], axis=0)
    b_low = jnp.concatenate([low[p, :, :COLS], low[p, :, COLS:]], axis=0)
    return mm(x_high, b_high) + (mm(x_low, b_high) + mm(x_high, b_low))


def packed(fields):
    group = lax.broadcasted_iota(I32, (STRIP, COLS), 1) // STRIP

    def rolled(value, shift):
        return pltpu.roll(value, shift % COLS, 1) if shift % COLS else value

    packs = []
    for base in (COLS - STRIP, 0):
        tops = [rolled(field[:PACKED], STRIP * l - base) for l, field in enumerate(fields)]
        blocks = []
        for i in range(PACKED // STRIP):
            block = tops[0][i * STRIP : (i + 1) * STRIP]
            for l in range(1, OWN):
                block = jnp.where(group == l, tops[l][i * STRIP : (i + 1) * STRIP], block)
            for q in range(2):
                tail = rolled(fields[2 * i + q][PACKED:], STRIP * (OWN + q) - base)
                block = jnp.where(group == OWN + q, tail, block)
            blocks.append(block)
        packs.append(jnp.concatenate(blocks, axis=0))
    return packs


def rows_at(v):
    return pl.ds(pl.multiple_of(v * PACKED, 8), PACKED)


def lat_body(
    nv, latitude, rows, before, after, near, far, high, low, out, last, lead, own_rows, far_rows
):
    y = latitude[0]
    planes = nv * OWN

    def strip(at, p, there):
        both = jnp.concatenate([at[p], at[planes + p]], axis=0)
        return jnp.where(there, both, 0.0)

    def one(v, carry):
        fields = []
        for l in range(OWN):
            p = v * OWN + l
            ends = strip(before, p, y > 0), strip(after, p, y < 3)
            fields.append(lat_filter(p, rows, *ends, high, low))
        for l in range(OWN):
            out[v * OWN + l] = fields[l]
        last[rows_at(v), :], lead[rows_at(v), :] = packed(fields)
        return carry

    lax.fori_loop(0, nv, one, 0)
    for d, (target, block) in enumerate(((own_rows, None), (last, nv), (lead, nv), (far_rows, None))):
        first = 2 * planes + 2 * d
        came = jnp.concatenate(
            [near[d], before[first : first + 2].reshape(PIECE, COLS)]
            + [far[d], after[first : first + 2].reshape(PIECE, COLS)],
            axis=0,
        )
        if block is None:
            target[...] = came
        else:
            target[nv * PACKED :, :] = came


def back_lat_body(nv, latitude, rows, before, after, high, low, out):
    y = latitude[0]

    def one(v, carry):
        for l in range(OWN):
            p = v * OWN + l
            ends = (
                jnp.where(y > 0, before[:, p].reshape(STRIP, COLS), 0.0),
                jnp.where(y < 3, after[:, p].reshape(STRIP, COLS), 0.0),
            )
            out[:, p] = lat_filter(p, rows, *ends, high, low).reshape(RINGS, 8, COLS)
        return carry

    lax.fori_loop(0, nv, one, 0)


def back_lon_body(nv, field, left, right, high, low, out):
    def one(v, carry):
        for l in range(OWN):
            p = v * OWN + l
            value = back_lon_filter(p, l, field[p], left[rows_at(v), :], right[rows_at(v), :], high, low)
            out[:, p] = value.reshape(RINGS, 8, COLS)
        return carry

    lax.fori_loop(0, nv, one, 0)


def observe_body(
    nv, field, left, right, own_rows, far_rows, high, low, weight,
    out, last, first, parts, values, misfit_high, misfit_low, row_hot, col_hot, col_hot2,
):
    came = pl.ds(nv * PACKED, 4 * PIECE)
    blocks = [own_rows[...], left[came, :], far_rows[...], right[came, :]]
    arrived(blocks, values, row_hot, col_hot, col_hot2)

    def filtered(v, carry):
        for l in range(OWN):
            p = v * OWN + l
            third = lon_filter(p, l, field[p], left[rows_at(v), :], right[rows_at(v), :], high, low)
            t_high, t_low = split(third)
            parts[p] = jnp.concatenate([t_high, t_low], axis=1)
        return carry

    lax.fori_loop(0, nv, filtered, 0)

    def gathered(v, carry):
        block = parts[pl.ds(v * OWN, OWN)].reshape(OWN * ROWS, 2 * COLS)
        across = mm(block, col_hot2[...])
        for l in range(OWN):
            p = v * OWN + l
            found = jnp.sum(across[l * ROWS : (l + 1) * ROWS] * row_hot[...], axis=0, keepdims=True)
            misfit = (found - values[p]) * jnp.concatenate([weight[p]] * 8, axis=1)
            m_high, m_low = split(misfit)
            misfit_high[p] = m_high.astype(F32)
            misfit_low[p] = m_low.astype(F32)
        return carry

    lax.fori_loop(0, nv, gathered, 0)

    def scattered(v, carry):
        placed = []
        for l in range(OWN):
            p = v * OWN + l
            placed.append((row_hot[...] * misfit_high[p]).astype(BF16))
            placed.append((row_hot[...] * misfit_low[p]).astype(BF16))
        both = mm_nt(jnp.concatenate(placed, axis=0), col_hot[...])
        fields = []
        for l in range(OWN):
            at = 2 * l * ROWS
            fields.append(both[at : at + ROWS] + both[at + ROWS : at + 2 * ROWS])
            out[v * OWN + l] = fields[-1]
        last[rows_at(v), :], first[rows_at(v), :] = packed(fields)
        return carry

    lax.fori_loop(0, nv, scattered, 0)


def route_body(core, longitude, latitude, kept, mate, tile, cell, out, by_lon, by_lat, by_both):
    c = core[0]
    count = tile.shape[1]
    east = ((tile[...] >> 2) - longitude[0]) & 3
    north = ((tile[...] & 3) - latitude[0]) & 3
    away = north * 4 + east
    hot = (lax.broadcasted_iota(I32, (TILES, count), 0) == away).astype(F32)
    earlier = lax.broadcasted_iota(I32, (count, count), 0) < lax.broadcasted_iota(I32, (count, count), 1)
    before = mm(hot.astype(BF16), earlier.astype(F32).astype(BF16))
    place = jnp.sum(before * hot, axis=0, keepdims=True).astype(I32)
    slot = away * SLOTS + place
    slot_hot = (lax.broadcasted_iota(I32, (TILES * SLOTS, count), 0) == slot).astype(F32).astype(BF16)
    observed = []
    for v in range(3):
        for part in range(2):
            for l in range(3):
                p = v * 3 + l
                observed.append(jnp.where(c == part, kept[p, :, 0:OBS], mate[p, :, 0:OBS]))
    sent = jnp.concatenate(
        observed + [(cell[...] + 1).astype(F32), jnp.zeros((5, count), F32)], axis=0
    )
    high, rest = split(sent)
    remainder = sent - high.astype(F32)
    low = (remainder - rest.astype(F32)).astype(BF16)
    all_parts = mm_nt(jnp.concatenate([high, rest, low], axis=0), slot_hot)
    full = all_parts[0:24] + (all_parts[24:48] + all_parts[48:72])
    lane = lax.broadcasted_iota(I32, (8, COLS), 1)
    for e in range(TILES // 2):
        at = slice(e * COLS, (e + 1) * COLS)
        a, b, c = full[0:8, at], full[8:16, at], full[16:24, at]
        a2, b2, c2 = [pltpu.roll(x, SLOTS, 1) for x in (a, b, c)]
        pair = (
            (jnp.where(lane < SLOTS, a, b2), jnp.where(lane < SLOTS, c, 0.0)),
            (jnp.where(lane < SLOTS, a2, b), jnp.where(lane < SLOTS, c2, 0.0)),
        )
        for i in range(2):
            north, east = e // 2, e % 2 * 2 + i
            y, x = (0, 1, None, 2)[north], (0, 1, None, 2)[east]
            if x is None:
                target = by_both if y is None else by_lon.at[y]
            else:
                target = by_lat.at[x] if y is None else out.at[y, x]
            target[0:8], target[8:16] = pair[i]


def arrived(blocks, values, row_hot, col_hot, col_hot2):
    low = lax.broadcasted_iota(I32, (8, COLS), 1) < SLOTS
    full = []
    for block in blocks:
        for first in (0, 2 * PIECE):
            a, c, b, d = [block[first + 8 * i : first + 8 * i + 8] for i in range(4)]
            full.append(
                jnp.concatenate(
                    [
                        jnp.where(low, a, pltpu.roll(b, SLOTS, 1)),
                        jnp.where(low, pltpu.roll(a, SLOTS, 1), b),
                        jnp.where(low, c, pltpu.roll(d, SLOTS, 1)),
                    ],
                    axis=0,
                )
            )
    full = jnp.concatenate(full, axis=1)
    for p in range(18):
        values[p] = full[p : p + 1]
    cell = full[18:19].astype(I32) - 1
    count = cell.shape[1]
    row_hot[...] = (lax.broadcasted_iota(I32, (ROWS, count), 0) == (cell >> 7)).astype(F32)
    cols = (lax.broadcasted_iota(I32, (COLS, count), 0) == (cell & 127)).astype(F32).astype(BF16)
    col_hot[...] = cols
    col_hot2[0:COLS] = cols
    col_hot2[COLS : 2 * COLS] = cols


def exchanged(last, first, axis):
    size = lax.axis_size(axis)
    up = [(i, (i + 1) % size) for i in range(size)]
    down = [(j, i) for i, j in up]
    return lax.ppermute(last, axis, up), lax.ppermute(first, axis, down)


def shifted(value, axis, by):
    size = lax.axis_size(axis)
    return lax.ppermute(value, axis, [(i, (i + by) % size) for i in range(size)])


def with_mate(value):
    pairs = [(i, i ^ 1) for i in range(lax.axis_size("lev"))]
    return lax.ppermute(value, "lev", pairs)


def over_rings(value):
    size = lax.axis_size("lev")
    groups = [list(range(0, size, 2)), list(range(1, size, 2))]
    return lax.all_to_all(value, "lev", 0, 0, tiled=True, axis_index_groups=groups)


def local(control, vertical, lon_taps, lat_taps, innovation, inv_variance, obs_tile, obs_cell):
    def index(axis):
        return lax.axis_index(axis).astype(I32).reshape(1)

    core, longitude, latitude = index("lev") % 2, index("lon"), index("lat")
    nv = 3
    planes = nv * OWN
    slots = TILES * SLOTS

    block, small_block = shape(9, ROWS, COLS), shape(9, 1, SMALL)
    kept, sent = kernel_call(begin_body, [block, block], [core, control], smem=(0,))
    arranged = kernel_call(
        arrange_body, [shape(RINGS, planes, 8, COLS)], [kept, with_mate(sent)]
    )[0]
    columns = over_rings(arranged)

    kept_small, sent_small = kernel_call(
        small_body,
        [small_block, small_block],
        [core, innovation, lon_taps, lat_taps, jnp.swapaxes(inv_variance, 0, 1)],
        smem=(0, 4),
        after=(arranged,),
    )
    mate_small = with_mate(sent_small)
    routed, by_lon, by_lat, by_both = kernel_call(
        route_body,
        [shape(3, 3, PIECE, COLS), shape(3, PIECE, COLS), shape(3, PIECE, COLS), shape(PIECE, COLS)],
        [core, longitude, latitude, kept_small, mate_small, obs_tile.reshape(1, -1), obs_cell.reshape(1, -1)],
        smem=(0, 1, 2),
        flops=2 * 72 * slots * obs_tile.shape[0],
    )
    n_lon, n_lat = lax.axis_size("lon"), lax.axis_size("lat")
    opposite = [
        (x * n_lat + y, (x + 2) % n_lon * n_lat + (y + 2) % n_lat)
        for x in range(n_lon)
        for y in range(n_lat)
    ]
    by_lon, by_lat = shifted(by_lon, "lon", 2), shifted(by_lat, "lat", 2)
    by_both = lax.ppermute(by_both, ("lon", "lat"), opposite)
    near, up, down = [jnp.concatenate([routed[i], by_lon[i : i + 1]], axis=0) for i in range(3)]
    far = jnp.concatenate([by_lat, by_both[None]], axis=0)
    first = over_rings(column_call(mix_body, core, columns, vertical, after=(far, near, up, down)))

    def with_rows(strips, rows):
        return jnp.concatenate([strips.reshape(-1, 8, COLS), rows.reshape(-1, 8, COLS)], axis=0)

    before, after = exchanged(
        with_rows(first[6:8], up), with_rows(first[0:2], down), "lat"
    )
    high, low, back_high, back_low, lon_high, lon_low, weight = kernel_call(
        bands_body,
        [shape(planes, ROWS, 128, dtype=BF16)] * 4
        + [shape(planes, COLS, 256, dtype=BF16)] * 2
        + [shape(planes, 1, 128)],
        [core, kept_small, mate_small],
        smem=(0,),
        flops=planes * 200000,
        after=(first,),
    )
    field_shape = shape(planes, ROWS, COLS)
    lat_flops = 2 * 3 * planes * ROWS * 128 * COLS
    row_block = shape(4 * PIECE, COLS)
    pack_rows = shape(nv * PACKED + 4 * PIECE, COLS)
    field, last, lead, own_rows, far_rows = kernel_call(
        functools.partial(lat_body, nv),
        [field_shape, pack_rows, pack_rows, row_block, row_block],
        [latitude, first, before, after, near, far, high, low],
        smem=(0,),
        flops=lat_flops,
    )
    left, right = exchanged(last, lead, "lon")
    pack_shape = shape(nv * PACKED, COLS)
    placed, last, lead = kernel_call(
        functools.partial(observe_body, nv),
        [field_shape, pack_shape, pack_shape],
        [field, left, right, own_rows, far_rows, lon_high, lon_low, weight],
        scratch=[
            pltpu.VMEM((planes, ROWS, 2 * COLS), BF16),
            pltpu.VMEM((planes, 1, slots), F32),
            pltpu.VMEM((planes, 1, slots), F32),
            pltpu.VMEM((planes, 1, slots), F32),
            pltpu.VMEM((ROWS, slots), F32),
            pltpu.VMEM((COLS, slots), BF16),
            pltpu.VMEM((2 * COLS, slots), BF16),
        ],
        flops=2 * planes * ROWS * slots * 256 * 2,
    )
    left, right = exchanged(last, lead, "lon")
    back = kernel_call(
        functools.partial(back_lon_body, nv),
        [shape(RINGS, planes, 8, COLS)],
        [placed, left, right, lon_high, lon_low],
        flops=2 * lat_flops,
    )[0]
    before, after = exchanged(back[6:8], back[0:2], "lat")
    back = kernel_call(
        functools.partial(back_lat_body, nv),
        [shape(RINGS, planes, 8, COLS)],
        [latitude, back, before, after, back_high, back_low],
        smem=(0,),
        flops=lat_flops,
    )[0]
    result = over_rings(column_call(unmix_body, core, over_rings(back), vertical, columns))

    mine, other = result[:, :9], with_mate(result[:, 9:])
    return kernel_call(
        finish_body,
        [shape(6, 3, ROWS, COLS)],
        [core, mine, other],
        smem=(0,),
    )[0]


def finish_body(core, mine, other, out):
    c = core[0]
    for v in range(3):
        for l in range(3):
            out[c * 3 + v, l] = mine[:, v * 3 + l].reshape(ROWS, COLS)
            out[(1 - c) * 3 + v, l] = other[:, v * 3 + l].reshape(ROWS, COLS)


def solution(mesh):
    return jax.shard_map(
        local,
        mesh=mesh,
        in_specs=(
            P(None, "lev", "lat", "lon"),
            P(),
            P(None, "lev", None),
            P(None, "lev", None),
            P(None, "lev", ("lon", "lat")),
            P(None, "lev"),
            P(("lon", "lat")),
            P(("lon", "lat")),
        ),
        out_specs=P(None, "lev", "lat", "lon"),
        check_vma=False,
    )
```

```python
import functools

import jax
import jax.numpy as jnp
from jax import lax
from jax.experimental import pallas as pl
from jax.experimental.pallas import tpu as pltpu
from jax.sharding import PartitionSpec as P

F32, BF16, I32 = jnp.float32, jnp.bfloat16, jnp.int32
ROWS, COLS = 64, 128
TAPS = 31
STRIP = 16
LEVELS = 48
RINGS = 8
OWN = 6
SLOTS = 64
TILES = 16
OBS = 512
LON_AT, LAT_AT, WEIGHT_AT, SMALL = OBS, OBS + 128, OBS + 256, OBS + 384
PIECE = 16
VMEM = pl.BlockSpec(memory_space=pltpu.VMEM)
SMEM = pl.BlockSpec(memory_space=pltpu.SMEM)


def kernel_call(body, outs, ins, scratch=(), smem=(), flops=0, limit=16, after=()):
    moved = sum(a.size * a.dtype.itemsize for a in ins)
    moved += sum(o.size * o.dtype.itemsize for o in outs)
    count = len(after)
    return pl.pallas_call(
        lambda *refs: body(*refs[count:]),
        out_shape=list(outs),
        in_specs=[pl.BlockSpec(memory_space=pl.ANY)] * count
        + [SMEM if i in smem else VMEM for i in range(len(ins))],
        out_specs=[VMEM] * len(outs),
        scratch_shapes=list(scratch),
        compiler_params=pltpu.CompilerParams(vmem_limit_bytes=limit * 2**20),
        cost_estimate=pl.CostEstimate(flops=flops, bytes_accessed=moved, transcendentals=0),
    )(*after, *ins)


def shape(*dims, dtype=F32):
    return jax.ShapeDtypeStruct(dims, dtype)


def split(value):
    high = value.astype(BF16)
    return high, (value - high.astype(F32)).astype(BF16)


def mm(a, b):
    return jnp.dot(a, b, preferred_element_type=F32)


def mm_nt(a, b):
    return lax.dot_general(a, b, (((1,), (1,)), ((), ())), preferred_element_type=F32)


def begin_body(core, control, kept, sent):
    c = core[0]
    for which, big in ((c, kept), (1 - c, sent)):
        for v in range(3):
            for l in range(3):
                big[v * 3 + l] = control[which * 3 + v, l]


def small_body(core, innovation, lon_taps, lat_taps, weight, kept, sent):
    c = core[0]
    kept[...] = jnp.zeros(kept.shape, F32)
    sent[...] = jnp.zeros(sent.shape, F32)
    for which, little in ((c, kept), (1 - c, sent)):
        for v in range(3):
            lon, lat, seen = [a[which * 3 + v] for a in (lon_taps, lat_taps, innovation)]
            for l in range(3):
                p = v * 3 + l
                little[p, :, 0:OBS] = seen[l : l + 1]
                little[p, :, LON_AT : LON_AT + TAPS] = lon[l : l + 1]
                little[p, :, LAT_AT : LAT_AT + TAPS] = lat[l : l + 1]
                little[p, :, WEIGHT_AT:] = jnp.full((1, 128), weight[l, which * 3 + v], F32)


def arrange_body(control, mate, out):
    for p in range(9):
        out[:, p] = control[p].reshape(RINGS, 8, COLS)
        out[:, 9 + p] = mate[p].reshape(RINGS, 8, COLS)


def rows_of(v, start, count):
    return pl.ds(v * LEVELS * 8 + start, count)


def mixed(matrix, held, v, side):
    at = [pl.ds(v * LEVELS * 8 + s, LEVELS, stride=8) for s in range(8)]
    columns = jnp.concatenate([held[a, :] for a in at], axis=1)
    result = lax.dot_general(
        matrix, columns, (((side,), (0,)), ((), ())),
        precision=lax.Precision.HIGHEST, preferred_element_type=F32,
    )
    for s in range(8):
        held[at[s], :] = result[:, s * COLS : (s + 1) * COLS]


def chip_order(c, part, own, mate):
    return jnp.where(c == part, own, mate)


def mix_body(core, got, matrix, out, held):
    c = core[0]
    for v in range(3):
        for s in range(RINGS):
            own, mate = got[s, v * 3 : v * 3 + 3], got[s, 9 + v * 3 : 12 + v * 3]
            for part in range(2):
                value = chip_order(c, part, own, mate)
                held[rows_of(v, s * 48 + part * 24, 24), :] = value.reshape(24, COLS)
        mixed(matrix[c * 3 + v], held, v, 1)
        for s in range(RINGS):
            out[s, v * OWN : (v + 1) * OWN] = held[rows_of(v, s * 48, 48), :].reshape(OWN, 8, COLS)


def unmix_body(core, got, matrix, control, out, held):
    c = core[0]
    for v in range(3):
        for s in range(RINGS):
            held[rows_of(v, s * 48, 48), :] = got[s, v * OWN : (v + 1) * OWN].reshape(48, COLS)
        mixed(matrix[c * 3 + v], held, v, 0)
        for s in range(RINGS):
            lower, upper = [held[rows_of(v, s * 48 + h * 24, 24), :].reshape(3, 8, COLS) for h in range(2)]
            for t in range(2):
                first = t * 9 + v * 3
                part = chip_order(c, t, lower, upper)
                out[s, first : first + 3] = part + control[s, first : first + 3]


def column_call(body, *ins, after=()):
    return kernel_call(
        body,
        [shape(*ins[1].shape)],
        ins,
        scratch=[pltpu.VMEM((3 * LEVELS * 8, COLS), F32)],
        smem=(0,),
        flops=2 * 3 * LEVELS * LEVELS * 1024 * 6,
        after=after,
    )[0]


def bands_body(core, kept, mate, high, low, back_high, back_low, lon_high, lon_low, weight):
    c = core[0]

    def toeplitz(row, height):
        full = jnp.broadcast_to(row, (height, row.shape[1]))
        return pltpu.roll(full, row.shape[1] - 15, 1, stride=1, stride_axis=0)

    def one(v, carry):
        for l in range(3):
            mine, other = kept[v * 3 + l], mate[v * 3 + l]
            for part in range(2):
                row = jnp.where(c == part, mine, other)
                p = v * OWN + part * 3 + l
                lat = toeplitz(row[:, LAT_AT : LAT_AT + 128], COLS)
                high[p], low[p] = split(lat[:ROWS])
                back_high[p], back_low[p] = split(lat.T[:ROWS])
                lon = jnp.concatenate([row[:, LON_AT : LON_AT + 128], jnp.zeros((1, 128), F32)], axis=1)
                lon_high[p], lon_low[p] = split(toeplitz(lon, COLS))
                weight[p] = row[:, WEIGHT_AT:]
        return carry

    lax.fori_loop(0, 3, one, 0, unroll=True)


def lat_filter(p, rows, before, after, high, low):
    extended = jnp.concatenate(
        [rows[:, p].reshape(ROWS, COLS), after, jnp.zeros((32, COLS), F32), before], axis=0
    )
    e_high, e_low = split(extended)
    return mm(high[p], e_high) + (mm(high[p], e_low) + mm(low[p], e_high))


PACKED = 48


def unpacked(pack, l, base):
    block = pack[l // 2 * STRIP : (l // 2 + 1) * STRIP]
    return jnp.concatenate(
        [
            pltpu.roll(pack, (base - STRIP * l) % COLS, 1) if (base - STRIP * l) % COLS else pack,
            pltpu.roll(block, (base - STRIP * (OWN + l % 2)) % COLS, 1),
        ],
        axis=0,
    )


def with_halo(l, field, left, right):
    lane = lax.broadcasted_iota(I32, (ROWS, COLS), 1)
    left, right = unpacked(left, l, COLS - STRIP), unpacked(right, l, 0)
    halo = jnp.where(lane >= COLS - STRIP, left, jnp.where(lane < STRIP, right, 0.0))
    return split(jnp.concatenate([field, halo], axis=1))


def lon_filter(p, l, field, left, right, high, low):
    x_high, x_low = with_halo(l, field, left, right)
    return mm_nt(x_high, high[p]) + (mm_nt(x_low, high[p]) + mm_nt(x_high, low[p]))


def back_lon_filter(p, l, field, left, right, high, low):
    x_high, x_low = with_halo(l, field, left, right)
    b_high = jnp.concatenate([high[p, :, :COLS], high[p, :, COLS:]], axis=0)
    b_low = jnp.concatenate([low[p, :, :COLS], low[p, :, COLS:]], axis=0)
    return mm(x_high, b_high) + (mm(x_low, b_high) + mm(x_high, b_low))


def packed(fields):
    group = lax.broadcasted_iota(I32, (STRIP, COLS), 1) // STRIP

    def rolled(value, shift):
        return pltpu.roll(value, shift % COLS, 1) if shift % COLS else value

    packs = []
    for base in (COLS - STRIP, 0):
        tops = [rolled(field[:PACKED], STRIP * l - base) for l, field in enumerate(fields)]
        blocks = []
        for i in range(PACKED // STRIP):
            block = tops[0][i * STRIP : (i + 1) * STRIP]
            for l in range(1, OWN):
                block = jnp.where(group == l, tops[l][i * STRIP : (i + 1) * STRIP], block)
            for q in range(2):
                tail = rolled(fields[2 * i + q][PACKED:], STRIP * (OWN + q) - base)
                block = jnp.where(group == OWN + q, tail, block)
            blocks.append(block)
        packs.append(jnp.concatenate(blocks, axis=0))
    return packs


def rows_at(v):
    return pl.ds(pl.multiple_of(v * PACKED, 8), PACKED)


def lat_body(
    nv, latitude, rows, before, after, near, far, high, low, out, last, lead, own_rows, far_rows
):
    y = latitude[0]
    planes = nv * OWN

    def strip(at, p, there):
        both = jnp.concatenate([at[p], at[planes + p]], axis=0)
        return jnp.where(there, both, 0.0)

    def one(v, carry):
        fields = []
        for l in range(OWN):
            p = v * OWN + l
            ends = strip(before, p, y > 0), strip(after, p, y < 3)
            fields.append(lat_filter(p, rows, *ends, high, low))
        for l in range(OWN):
            out[v * OWN + l] = fields[l]
        last[rows_at(v), :], lead[rows_at(v), :] = packed(fields)
        return carry

    lax.fori_loop(0, nv, one, 0, unroll=True)
    for d, (target, block) in enumerate(((own_rows, None), (last, nv), (lead, nv), (far_rows, None))):
        first = 2 * planes + 2 * d
        came = jnp.concatenate(
            [near[d], before[first : first + 2].reshape(PIECE, COLS)]
            + [far[d], after[first : first + 2].reshape(PIECE, COLS)],
            axis=0,
        )
        if block is None:
            target[...] = came
        else:
            target[nv * PACKED :, :] = came


def back_lat_body(nv, latitude, rows, before, after, high, low, out):
    y = latitude[0]

    def one(v, carry):
        for l in range(OWN):
            p = v * OWN + l
            ends = (
                jnp.where(y > 0, before[:, p].reshape(STRIP, COLS), 0.0),
                jnp.where(y < 3, after[:, p].reshape(STRIP, COLS), 0.0),
            )
            out[:, p] = lat_filter(p, rows, *ends, high, low).reshape(RINGS, 8, COLS)
        return carry

    lax.fori_loop(0, nv, one, 0, unroll=True)


def back_lon_body(nv, field, left, right, high, low, out):
    def one(v, carry):
        for l in range(OWN):
            p = v * OWN + l
            value = back_lon_filter(p, l, field[p], left[rows_at(v), :], right[rows_at(v), :], high, low)
            out[:, p] = value.reshape(RINGS, 8, COLS)
        return carry

    lax.fori_loop(0, nv, one, 0, unroll=True)


def observe_body(
    nv, field, left, right, own_rows, far_rows, high, low, weight,
    out, last, first, parts, values, misfit_high, misfit_low, row_hot, col_hot, col_hot2,
):
    came = pl.ds(nv * PACKED, 4 * PIECE)
    blocks = [own_rows[...], left[came, :], far_rows[...], right[came, :]]
    arrived(blocks, values, row_hot, col_hot, col_hot2)

    def filtered(v, carry):
        for l in range(OWN):
            p = v * OWN + l
            third = lon_filter(p, l, field[p], left[rows_at(v), :], right[rows_at(v), :], high, low)
            t_high, t_low = split(third)
            parts[p] = jnp.concatenate([t_high, t_low], axis=1)
        return carry

    lax.fori_loop(0, nv, filtered, 0, unroll=True)

    def gathered(v, carry):
        block = parts[pl.ds(v * OWN, OWN)].reshape(OWN * ROWS, 2 * COLS)
        across = mm(block, col_hot2[...])
        for l in range(OWN):
            p = v * OWN + l
            found = jnp.sum(across[l * ROWS : (l + 1) * ROWS] * row_hot[...], axis=0, keepdims=True)
            misfit = (found - values[p]) * jnp.concatenate([weight[p]] * 8, axis=1)
            m_high, m_low = split(misfit)
            misfit_high[p] = m_high.astype(F32)
            misfit_low[p] = m_low.astype(F32)
        return carry

    lax.fori_loop(0, nv, gathered, 0, unroll=True)

    def scattered(v, carry):
        placed = []
        for l in range(OWN):
            p = v * OWN + l
            placed.append((row_hot[...] * misfit_high[p]).astype(BF16))
            placed.append((row_hot[...] * misfit_low[p]).astype(BF16))
        both = mm_nt(jnp.concatenate(placed, axis=0), col_hot[...])
        fields = []
        for l in range(OWN):
            at = 2 * l * ROWS
            fields.append(both[at : at + ROWS] + both[at + ROWS : at + 2 * ROWS])
            out[v * OWN + l] = fields[-1]
        last[rows_at(v), :], first[rows_at(v), :] = packed(fields)
        return carry

    lax.fori_loop(0, nv, scattered, 0, unroll=True)


def route_body(core, longitude, latitude, kept, mate, tile, cell, out, by_lon, by_lat, by_both):
    c = core[0]
    count = tile.shape[1]
    east = ((tile[...] >> 2) - longitude[0]) & 3
    north = ((tile[...] & 3) - latitude[0]) & 3
    away = north * 4 + east
    hot = (lax.broadcasted_iota(I32, (TILES, count), 0) == away).astype(F32)
    earlier = lax.broadcasted_iota(I32, (count, count), 0) < lax.broadcasted_iota(I32, (count, count), 1)
    before = mm(hot.astype(BF16), earlier.astype(F32).astype(BF16))
    place = jnp.sum(before * hot, axis=0, keepdims=True).astype(I32)
    slot = away * SLOTS + place
    slot_hot = (lax.broadcasted_iota(I32, (TILES * SLOTS, count), 0) == slot).astype(F32).astype(BF16)
    observed = []
    for v in range(3):
        for part in range(2):
            for l in range(3):
                p = v * 3 + l
                observed.append(jnp.where(c == part, kept[p, :, 0:OBS], mate[p, :, 0:OBS]))
    sent = jnp.concatenate(
        observed + [(cell[...] + 1).astype(F32), jnp.zeros((5, count), F32)], axis=0
    )
    high, rest = split(sent)
    remainder = sent - high.astype(F32)
    low = (remainder - rest.astype(F32)).astype(BF16)
    all_parts = mm_nt(jnp.concatenate([high, rest, low], axis=0), slot_hot)
    full = all_parts[0:24] + (all_parts[24:48] + all_parts[48:72])
    lane = lax.broadcasted_iota(I32, (8, COLS), 1)
    for e in range(TILES // 2):
        at = slice(e * COLS, (e + 1) * COLS)
        a, b, c = full[0:8, at], full[8:16, at], full[16:24, at]
        a2, b2, c2 = [pltpu.roll(x, SLOTS, 1) for x in (a, b, c)]
        pair = (
            (jnp.where(lane < SLOTS, a, b2), jnp.where(lane < SLOTS, c, 0.0)),
            (jnp.where(lane < SLOTS, a2, b), jnp.where(lane < SLOTS, c2, 0.0)),
        )
        for i in range(2):
            north, east = e // 2, e % 2 * 2 + i
            y, x = (0, 1, None, 2)[north], (0, 1, None, 2)[east]
            if x is None:
                target = by_both if y is None else by_lon.at[y]
            else:
                target = by_lat.at[x] if y is None else out.at[y, x]
            target[0:8], target[8:16] = pair[i]


def arrived(blocks, values, row_hot, col_hot, col_hot2):
    low = lax.broadcasted_iota(I32, (8, COLS), 1) < SLOTS
    full = []
    for block in blocks:
        for first in (0, 2 * PIECE):
            a, c, b, d = [block[first + 8 * i : first + 8 * i + 8] for i in range(4)]
            full.append(
                jnp.concatenate(
                    [
                        jnp.where(low, a, pltpu.roll(b, SLOTS, 1)),
                        jnp.where(low, pltpu.roll(a, SLOTS, 1), b),
                        jnp.where(low, c, pltpu.roll(d, SLOTS, 1)),
                    ],
                    axis=0,
                )
            )
    full = jnp.concatenate(full, axis=1)
    for p in range(18):
        values[p] = full[p : p + 1]
    cell = full[18:19].astype(I32) - 1
    count = cell.shape[1]
    row_hot[...] = (lax.broadcasted_iota(I32, (ROWS, count), 0) == (cell >> 7)).astype(F32)
    cols = (lax.broadcasted_iota(I32, (COLS, count), 0) == (cell & 127)).astype(F32).astype(BF16)
    col_hot[...] = cols
    col_hot2[0:COLS] = cols
    col_hot2[COLS : 2 * COLS] = cols


def exchanged(last, first, axis):
    size = lax.axis_size(axis)
    up = [(i, (i + 1) % size) for i in range(size)]
    down = [(j, i) for i, j in up]
    return lax.ppermute(last, axis, up), lax.ppermute(first, axis, down)


def shifted(value, axis, by):
    size = lax.axis_size(axis)
    return lax.ppermute(value, axis, [(i, (i + by) % size) for i in range(size)])


def with_mate(value):
    pairs = [(i, i ^ 1) for i in range(lax.axis_size("lev"))]
    return lax.ppermute(value, "lev", pairs)


def over_rings(value):
    size = lax.axis_size("lev")
    groups = [list(range(0, size, 2)), list(range(1, size, 2))]
    return lax.all_to_all(value, "lev", 0, 0, tiled=True, axis_index_groups=groups)


def local(control, vertical, lon_taps, lat_taps, innovation, inv_variance, obs_tile, obs_cell):
    def index(axis):
        return lax.axis_index(axis).astype(I32).reshape(1)

    core, longitude, latitude = index("lev") % 2, index("lon"), index("lat")
    nv = 3
    planes = nv * OWN
    slots = TILES * SLOTS

    block, small_block = shape(9, ROWS, COLS), shape(9, 1, SMALL)
    kept, sent = kernel_call(begin_body, [block, block], [core, control], smem=(0,))
    arranged = kernel_call(
        arrange_body, [shape(RINGS, planes, 8, COLS)], [kept, with_mate(sent)]
    )[0]
    columns = over_rings(arranged)

    kept_small, sent_small = kernel_call(
        small_body,
        [small_block, small_block],
        [core, innovation, lon_taps, lat_taps, jnp.swapaxes(inv_variance, 0, 1)],
        smem=(0, 4),
        after=(arranged,),
    )
    mate_small = with_mate(sent_small)
    routed, by_lon, by_lat, by_both = kernel_call(
        route_body,
        [shape(3, 3, PIECE, COLS), shape(3, PIECE, COLS), shape(3, PIECE, COLS), shape(PIECE, COLS)],
        [core, longitude, latitude, kept_small, mate_small, obs_tile.reshape(1, -1), obs_cell.reshape(1, -1)],
        smem=(0, 1, 2),
        flops=2 * 72 * slots * obs_tile.shape[0],
    )
    n_lon, n_lat = lax.axis_size("lon"), lax.axis_size("lat")
    opposite = [
        (x * n_lat + y, (x + 2) % n_lon * n_lat + (y + 2) % n_lat)
        for x in range(n_lon)
        for y in range(n_lat)
    ]
    by_lon, by_lat = shifted(by_lon, "lon", 2), shifted(by_lat, "lat", 2)
    by_both = lax.ppermute(by_both, ("lon", "lat"), opposite)
    near, up, down = [jnp.concatenate([routed[i], by_lon[i : i + 1]], axis=0) for i in range(3)]
    far = jnp.concatenate([by_lat, by_both[None]], axis=0)
    first = over_rings(column_call(mix_body, core, columns, vertical, after=(far, near, up, down)))

    def with_rows(strips, rows):
        return jnp.concatenate([strips.reshape(-1, 8, COLS), rows.reshape(-1, 8, COLS)], axis=0)

    before, after = exchanged(
        with_rows(first[6:8], up), with_rows(first[0:2], down), "lat"
    )
    high, low, back_high, back_low, lon_high, lon_low, weight = kernel_call(
        bands_body,
        [shape(planes, ROWS, 128, dtype=BF16)] * 4
        + [shape(planes, COLS, 256, dtype=BF16)] * 2
        + [shape(planes, 1, 128)],
        [core, kept_small, mate_small],
        smem=(0,),
        flops=planes * 200000,
        after=(first,),
    )
    field_shape = shape(planes, ROWS, COLS)
    lat_flops = 2 * 3 * planes * ROWS * 128 * COLS
    row_block = shape(4 * PIECE, COLS)
    pack_rows = shape(nv * PACKED + 4 * PIECE, COLS)
    field, last, lead, own_rows, far_rows = kernel_call(
        functools.partial(lat_body, nv),
        [field_shape, pack_rows, pack_rows, row_block, row_block],
        [latitude, first, before, after, near, far, high, low],
        smem=(0,),
        flops=lat_flops,
    )
    left, right = exchanged(last, lead, "lon")
    pack_shape = shape(nv * PACKED, COLS)
    placed, last, lead = kernel_call(
        functools.partial(observe_body, nv),
        [field_shape, pack_shape, pack_shape],
        [field, left, right, own_rows, far_rows, lon_high, lon_low, weight],
        scratch=[
            pltpu.VMEM((planes, ROWS, 2 * COLS), BF16),
            pltpu.VMEM((planes, 1, slots), F32),
            pltpu.VMEM((planes, 1, slots), F32),
            pltpu.VMEM((planes, 1, slots), F32),
            pltpu.VMEM((ROWS, slots), F32),
            pltpu.VMEM((COLS, slots), BF16),
            pltpu.VMEM((2 * COLS, slots), BF16),
        ],
        flops=2 * planes * ROWS * slots * 256 * 2,
    )
    left, right = exchanged(last, lead, "lon")
    back = kernel_call(
        functools.partial(back_lon_body, nv),
        [shape(RINGS, planes, 8, COLS)],
        [placed, left, right, lon_high, lon_low],
        flops=2 * lat_flops,
    )[0]
    before, after = exchanged(back[6:8], back[0:2], "lat")
    back = kernel_call(
        functools.partial(back_lat_body, nv),
        [shape(RINGS, planes, 8, COLS)],
        [latitude, back, before, after, back_high, back_low],
        smem=(0,),
        flops=lat_flops,
    )[0]
    result = over_rings(column_call(unmix_body, core, over_rings(back), vertical, columns))

    mine, other = result[:, :9], with_mate(result[:, 9:])
    return kernel_call(
        finish_body,
        [shape(6, 3, ROWS, COLS)],
        [core, mine, other],
        smem=(0,),
    )[0]


def finish_body(core, mine, other, out):
    c = core[0]
    for v in range(3):
        for l in range(3):
            out[c * 3 + v, l] = mine[:, v * 3 + l].reshape(ROWS, COLS)
            out[(1 - c) * 3 + v, l] = other[:, v * 3 + l].reshape(ROWS, COLS)


def solution(mesh):
    return jax.shard_map(
        local,
        mesh=mesh,
        in_specs=(
            P(None, "lev", "lat", "lon"),
            P(),
            P(None, "lev", None),
            P(None, "lev", None),
            P(None, "lev", ("lon", "lat")),
            P(None, "lev"),
            P(("lon", "lat")),
            P(("lon", "lat")),
        ),
        out_specs=P(None, "lev", "lat", "lon"),
        check_vma=False,
    )
```

```python
import functools

import jax
import jax.numpy as jnp
from jax import lax
from jax.experimental import pallas as pl
from jax.experimental.pallas import tpu as pltpu
from jax.sharding import PartitionSpec as P

F32, BF16, I32 = jnp.float32, jnp.bfloat16, jnp.int32
ROWS, COLS = 64, 128
TAPS = 31
STRIP = 16
LEVELS = 48
RINGS = 8
OWN = 6
SLOTS = 64
TILES = 16
OBS = 512
LON_AT, LAT_AT, WEIGHT_AT, SMALL = OBS, OBS + 128, OBS + 256, OBS + 384
PIECE = 16
VMEM = pl.BlockSpec(memory_space=pltpu.VMEM)
SMEM = pl.BlockSpec(memory_space=pltpu.SMEM)


def kernel_call(body, outs, ins, scratch=(), smem=(), flops=0, limit=16, after=()):
    moved = sum(a.size * a.dtype.itemsize for a in ins)
    moved += sum(o.size * o.dtype.itemsize for o in outs)
    count = len(after)
    return pl.pallas_call(
        lambda *refs: body(*refs[count:]),
        out_shape=list(outs),
        in_specs=[pl.BlockSpec(memory_space=pl.ANY)] * count
        + [SMEM if i in smem else VMEM for i in range(len(ins))],
        out_specs=[VMEM] * len(outs),
        scratch_shapes=list(scratch),
        compiler_params=pltpu.CompilerParams(vmem_limit_bytes=limit * 2**20),
        cost_estimate=pl.CostEstimate(flops=flops, bytes_accessed=moved, transcendentals=0),
    )(*after, *ins)


def shape(*dims, dtype=F32):
    return jax.ShapeDtypeStruct(dims, dtype)


def split(value):
    high = value.astype(BF16)
    return high, (value - high.astype(F32)).astype(BF16)


def mm(a, b):
    return jnp.dot(a, b, preferred_element_type=F32)


def mm_nt(a, b):
    return lax.dot_general(a, b, (((1,), (1,)), ((), ())), preferred_element_type=F32)


def begin_body(core, control, kept, sent):
    c = core[0]
    for which, big in ((c, kept), (1 - c, sent)):
        for v in range(3):
            for l in range(3):
                big[v * 3 + l] = control[which * 3 + v, l]


def small_body(core, innovation, lon_taps, lat_taps, weight, kept, sent):
    c = core[0]
    kept[...] = jnp.zeros(kept.shape, F32)
    sent[...] = jnp.zeros(sent.shape, F32)
    for which, little in ((c, kept), (1 - c, sent)):
        for v in range(3):
            lon, lat, seen = [a[which * 3 + v] for a in (lon_taps, lat_taps, innovation)]
            for l in range(3):
                p = v * 3 + l
                little[p, :, 0:OBS] = seen[l : l + 1]
                little[p, :, LON_AT : LON_AT + TAPS] = lon[l : l + 1]
                little[p, :, LAT_AT : LAT_AT + TAPS] = lat[l : l + 1]
                little[p, :, WEIGHT_AT:] = jnp.full((1, 128), weight[l, which * 3 + v], F32)


def arrange_body(control, mate, out):
    for p in range(9):
        out[:, p] = control[p].reshape(RINGS, 8, COLS)
        out[:, 9 + p] = mate[p].reshape(RINGS, 8, COLS)


def rows_of(v, start, count):
    return pl.ds(v * LEVELS * 8 + start, count)


def mixed(matrix, held, v, side):
    at = [pl.ds(v * LEVELS * 8 + s, LEVELS, stride=8) for s in range(8)]
    columns = jnp.concatenate([held[a, :] for a in at], axis=1)
    (m_high, m_low), (c_high, c_low) = split(matrix.T if side == 0 else matrix), split(columns)
    result = mm(m_high, c_high) + (mm(m_high, c_low) + mm(m_low, c_high))
    for s in range(8):
        held[at[s], :] = result[:, s * COLS : (s + 1) * COLS]


def chip_order(c, part, own, mate):
    return jnp.where(c == part, own, mate)


def mix_body(core, got, matrix, out, held):
    c = core[0]
    for v in range(3):
        for s in range(RINGS):
            own, mate = got[s, v * 3 : v * 3 + 3], got[s, 9 + v * 3 : 12 + v * 3]
            for part in range(2):
                value = chip_order(c, part, own, mate)
                held[rows_of(v, s * 48 + part * 24, 24), :] = value.reshape(24, COLS)
        mixed(matrix[c * 3 + v], held, v, 1)
        for s in range(RINGS):
            out[s, v * OWN : (v + 1) * OWN] = held[rows_of(v, s * 48, 48), :].reshape(OWN, 8, COLS)


def unmix_body(core, got, matrix, control, out, held):
    c = core[0]
    for v in range(3):
        for s in range(RINGS):
            held[rows_of(v, s * 48, 48), :] = got[s, v * OWN : (v + 1) * OWN].reshape(48, COLS)
        mixed(matrix[c * 3 + v], held, v, 0)
        for s in range(RINGS):
            lower, upper = [held[rows_of(v, s * 48 + h * 24, 24), :].reshape(3, 8, COLS) for h in range(2)]
            for t in range(2):
                first = t * 9 + v * 3
                part = chip_order(c, t, lower, upper)
                out[s, first : first + 3] = part + control[s, first : first + 3]


def column_call(body, *ins, after=()):
    return kernel_call(
        body,
        [shape(*ins[1].shape)],
        ins,
        scratch=[pltpu.VMEM((3 * LEVELS * 8, COLS), F32)],
        smem=(0,),
        flops=2 * 3 * LEVELS * LEVELS * 1024 * 6,
        after=after,
    )[0]


def bands_body(core, kept, mate, high, low, back_high, back_low, lon_high, lon_low, weight):
    c = core[0]

    def toeplitz(row, height):
        full = jnp.broadcast_to(row, (height, row.shape[1]))
        return pltpu.roll(full, row.shape[1] - 15, 1, stride=1, stride_axis=0)

    def one(v, carry):
        for l in range(3):
            mine, other = kept[v * 3 + l], mate[v * 3 + l]
            for part in range(2):
                row = jnp.where(c == part, mine, other)
                p = v * OWN + part * 3 + l
                lat = toeplitz(row[:, LAT_AT : LAT_AT + 128], COLS)
                high[p], low[p] = split(lat[:ROWS])
                back_high[p], back_low[p] = split(lat.T[:ROWS])
                lon = jnp.concatenate([row[:, LON_AT : LON_AT + 128], jnp.zeros((1, 128), F32)], axis=1)
                lon_high[p], lon_low[p] = split(toeplitz(lon, COLS))
                weight[p] = row[:, WEIGHT_AT:]
        return carry

    lax.fori_loop(0, 3, one, 0, unroll=True)


def lat_filter(p, rows, before, after, high, low):
    extended = jnp.concatenate(
        [rows[:, p].reshape(ROWS, COLS), after, jnp.zeros((32, COLS), F32), before], axis=0
    )
    e_high, e_low = split(extended)
    return mm(high[p], e_high) + (mm(high[p], e_low) + mm(low[p], e_high))


PACKED = 48


def unpacked(pack, l, base):
    block = pack[l // 2 * STRIP : (l // 2 + 1) * STRIP]
    return jnp.concatenate(
        [
            pltpu.roll(pack, (base - STRIP * l) % COLS, 1) if (base - STRIP * l) % COLS else pack,
            pltpu.roll(block, (base - STRIP * (OWN + l % 2)) % COLS, 1),
        ],
        axis=0,
    )


def with_halo(l, field, left, right):
    lane = lax.broadcasted_iota(I32, (ROWS, COLS), 1)
    left, right = unpacked(left, l, COLS - STRIP), unpacked(right, l, 0)
    halo = jnp.where(lane >= COLS - STRIP, left, jnp.where(lane < STRIP, right, 0.0))
    return split(jnp.concatenate([field, halo], axis=1))


def lon_filter(p, l, field, left, right, high, low):
    x_high, x_low = with_halo(l, field, left, right)
    return mm_nt(x_high, high[p]) + (mm_nt(x_low, high[p]) + mm_nt(x_high, low[p]))


def back_lon_filter(p, l, field, left, right, high, low):
    x_high, x_low = with_halo(l, field, left, right)
    b_high = jnp.concatenate([high[p, :, :COLS], high[p, :, COLS:]], axis=0)
    b_low = jnp.concatenate([low[p, :, :COLS], low[p, :, COLS:]], axis=0)
    return mm(x_high, b_high) + (mm(x_low, b_high) + mm(x_high, b_low))


def packed(fields):
    group = lax.broadcasted_iota(I32, (STRIP, COLS), 1) // STRIP

    def rolled(value, shift):
        return pltpu.roll(value, shift % COLS, 1) if shift % COLS else value

    packs = []
    for base in (COLS - STRIP, 0):
        tops = [rolled(field[:PACKED], STRIP * l - base) for l, field in enumerate(fields)]
        blocks = []
        for i in range(PACKED // STRIP):
            block = tops[0][i * STRIP : (i + 1) * STRIP]
            for l in range(1, OWN):
                block = jnp.where(group == l, tops[l][i * STRIP : (i + 1) * STRIP], block)
            for q in range(2):
                tail = rolled(fields[2 * i + q][PACKED:], STRIP * (OWN + q) - base)
                block = jnp.where(group == OWN + q, tail, block)
            blocks.append(block)
        packs.append(jnp.concatenate(blocks, axis=0))
    return packs


def rows_at(v):
    return pl.ds(pl.multiple_of(v * PACKED, 8), PACKED)


def lat_body(
    nv, latitude, rows, before, after, near, far, high, low, out, last, lead, own_rows, far_rows
):
    y = latitude[0]
    planes = nv * OWN

    def strip(at, p, there):
        both = jnp.concatenate([at[p], at[planes + p]], axis=0)
        return jnp.where(there, both, 0.0)

    def one(v, carry):
        fields = []
        for l in range(OWN):
            p = v * OWN + l
            ends = strip(before, p, y > 0), strip(after, p, y < 3)
            fields.append(lat_filter(p, rows, *ends, high, low))
        for l in range(OWN):
            out[v * OWN + l] = fields[l]
        last[rows_at(v), :], lead[rows_at(v), :] = packed(fields)
        return carry

    lax.fori_loop(0, nv, one, 0, unroll=True)
    for d, (target, block) in enumerate(((own_rows, None), (last, nv), (lead, nv), (far_rows, None))):
        first = 2 * planes + 2 * d
        came = jnp.concatenate(
            [near[d], before[first : first + 2].reshape(PIECE, COLS)]
            + [far[d], after[first : first + 2].reshape(PIECE, COLS)],
            axis=0,
        )
        if block is None:
            target[...] = came
        else:
            target[nv * PACKED :, :] = came


def back_lat_body(nv, latitude, rows, before, after, high, low, out):
    y = latitude[0]

    def one(v, carry):
        for l in range(OWN):
            p = v * OWN + l
            ends = (
                jnp.where(y > 0, before[:, p].reshape(STRIP, COLS), 0.0),
                jnp.where(y < 3, after[:, p].reshape(STRIP, COLS), 0.0),
            )
            out[:, p] = lat_filter(p, rows, *ends, high, low).reshape(RINGS, 8, COLS)
        return carry

    lax.fori_loop(0, nv, one, 0, unroll=True)


def back_lon_body(nv, field, left, right, high, low, out, last, lead):
    def one(v, carry):
        for l in range(OWN):
            p = v * OWN + l
            value = back_lon_filter(p, l, field[p], left[rows_at(v), :], right[rows_at(v), :], high, low)
            out[:, p] = value.reshape(RINGS, 8, COLS)
            last[:, p] = value[ROWS - STRIP :].reshape(2, 8, COLS)
            lead[:, p] = value[:STRIP].reshape(2, 8, COLS)
        return carry

    lax.fori_loop(0, nv, one, 0, unroll=True)


def observe_body(
    nv, field, left, right, own_rows, far_rows, high, low, weight,
    out, last, first, parts, values, misfit_high, misfit_low, row_hot, col_hot, col_hot2,
):
    came = pl.ds(nv * PACKED, 4 * PIECE)
    blocks = [own_rows[...], left[came, :], far_rows[...], right[came, :]]
    arrived(blocks, values, row_hot, col_hot, col_hot2)

    def filtered(v, carry):
        for l in range(OWN):
            p = v * OWN + l
            third = lon_filter(p, l, field[p], left[rows_at(v), :], right[rows_at(v), :], high, low)
            t_high, t_low = split(third)
            parts[p] = jnp.concatenate([t_high, t_low], axis=1)
        return carry

    lax.fori_loop(0, nv, filtered, 0, unroll=True)

    def gathered(v, carry):
        block = parts[pl.ds(v * OWN, OWN)].reshape(OWN * ROWS, 2 * COLS)
        across = mm(block, col_hot2[...])
        for l in range(OWN):
            p = v * OWN + l
            found = jnp.sum(across[l * ROWS : (l + 1) * ROWS] * row_hot[...], axis=0, keepdims=True)
            misfit = (found - values[p]) * jnp.concatenate([weight[p]] * 8, axis=1)
            m_high, m_low = split(misfit)
            misfit_high[p] = m_high.astype(F32)
            misfit_low[p] = m_low.astype(F32)
        return carry

    lax.fori_loop(0, nv, gathered, 0, unroll=True)

    def scattered(v, carry):
        placed = []
        for l in range(OWN):
            p = v * OWN + l
            placed.append((row_hot[...] * misfit_high[p]).astype(BF16))
            placed.append((row_hot[...] * misfit_low[p]).astype(BF16))
        both = mm_nt(jnp.concatenate(placed, axis=0), col_hot[...])
        fields = []
        for l in range(OWN):
            at = 2 * l * ROWS
            fields.append(both[at : at + ROWS] + both[at + ROWS : at + 2 * ROWS])
            out[v * OWN + l] = fields[-1]
        last[rows_at(v), :], first[rows_at(v), :] = packed(fields)
        return carry

    lax.fori_loop(0, nv, scattered, 0, unroll=True)


def route_body(core, longitude, latitude, kept, mate, tile, cell, out, by_lon, by_lat, by_both):
    c = core[0]
    count = tile.shape[1]
    east = ((tile[...] >> 2) - longitude[0]) & 3
    north = ((tile[...] & 3) - latitude[0]) & 3
    away = north * 4 + east
    hot = (lax.broadcasted_iota(I32, (TILES, count), 0) == away).astype(F32)
    earlier = lax.broadcasted_iota(I32, (count, count), 0) < lax.broadcasted_iota(I32, (count, count), 1)
    before = mm(hot.astype(BF16), earlier.astype(F32).astype(BF16))
    place = jnp.sum(before * hot, axis=0, keepdims=True).astype(I32)
    slot = away * SLOTS + place
    slot_hot = (lax.broadcasted_iota(I32, (TILES * SLOTS, count), 0) == slot).astype(F32).astype(BF16)
    observed = []
    for v in range(3):
        for part in range(2):
            for l in range(3):
                p = v * 3 + l
                observed.append(jnp.where(c == part, kept[p, :, 0:OBS], mate[p, :, 0:OBS]))
    sent = jnp.concatenate(
        observed + [(cell[...] + 1).astype(F32), jnp.zeros((5, count), F32)], axis=0
    )
    high, rest = split(sent)
    remainder = sent - high.astype(F32)
    low = (remainder - rest.astype(F32)).astype(BF16)
    all_parts = mm_nt(jnp.concatenate([high, rest, low], axis=0), slot_hot)
    full = all_parts[0:24] + (all_parts[24:48] + all_parts[48:72])
    lane = lax.broadcasted_iota(I32, (8, COLS), 1)
    for e in range(TILES // 2):
        at = slice(e * COLS, (e + 1) * COLS)
        a, b, c = full[0:8, at], full[8:16, at], full[16:24, at]
        a2, b2, c2 = [pltpu.roll(x, SLOTS, 1) for x in (a, b, c)]
        pair = (
            (jnp.where(lane < SLOTS, a, b2), jnp.where(lane < SLOTS, c, 0.0)),
            (jnp.where(lane < SLOTS, a2, b), jnp.where(lane < SLOTS, c2, 0.0)),
        )
        for i in range(2):
            north, east = e // 2, e % 2 * 2 + i
            y, x = (0, 1, None, 2)[north], (0, 1, None, 2)[east]
            if x is None:
                target = by_both if y is None else by_lon.at[y]
            else:
                target = by_lat.at[x] if y is None else out.at[y, x]
            target[0:8], target[8:16] = pair[i]


def arrived(blocks, values, row_hot, col_hot, col_hot2):
    low = lax.broadcasted_iota(I32, (8, COLS), 1) < SLOTS
    full = []
    for block in blocks:
        for first in (0, 2 * PIECE):
            a, c, b, d = [block[first + 8 * i : first + 8 * i + 8] for i in range(4)]
            full.append(
                jnp.concatenate(
                    [
                        jnp.where(low, a, pltpu.roll(b, SLOTS, 1)),
                        jnp.where(low, pltpu.roll(a, SLOTS, 1), b),
                        jnp.where(low, c, pltpu.roll(d, SLOTS, 1)),
                    ],
                    axis=0,
                )
            )
    full = jnp.concatenate(full, axis=1)
    for p in range(18):
        values[p] = full[p : p + 1]
    cell = full[18:19].astype(I32) - 1
    count = cell.shape[1]
    row_hot[...] = (lax.broadcasted_iota(I32, (ROWS, count), 0) == (cell >> 7)).astype(F32)
    cols = (lax.broadcasted_iota(I32, (COLS, count), 0) == (cell & 127)).astype(F32).astype(BF16)
    col_hot[...] = cols
    col_hot2[0:COLS] = cols
    col_hot2[COLS : 2 * COLS] = cols


def exchanged(last, first, axis):
    size = lax.axis_size(axis)
    up = [(i, (i + 1) % size) for i in range(size)]
    down = [(j, i) for i, j in up]
    return lax.ppermute(last, axis, up), lax.ppermute(first, axis, down)


def shifted(value, axis, by):
    size = lax.axis_size(axis)
    return lax.ppermute(value, axis, [(i, (i + by) % size) for i in range(size)])


def with_mate(value):
    pairs = [(i, i ^ 1) for i in range(lax.axis_size("lev"))]
    return lax.ppermute(value, "lev", pairs)


def over_rings(value):
    size = lax.axis_size("lev")
    groups = [list(range(0, size, 2)), list(range(1, size, 2))]
    return lax.all_to_all(value, "lev", 0, 0, tiled=True, axis_index_groups=groups)


def local(control, vertical, lon_taps, lat_taps, innovation, inv_variance, obs_tile, obs_cell):
    def index(axis):
        return lax.axis_index(axis).astype(I32).reshape(1)

    core, longitude, latitude = index("lev") % 2, index("lon"), index("lat")
    nv = 3
    planes = nv * OWN
    slots = TILES * SLOTS

    block, small_block = shape(9, ROWS, COLS), shape(9, 1, SMALL)
    kept, sent = kernel_call(begin_body, [block, block], [core, control], smem=(0,))
    arranged = kernel_call(
        arrange_body, [shape(RINGS, planes, 8, COLS)], [kept, with_mate(sent)]
    )[0]
    columns = over_rings(arranged)

    kept_small, sent_small = kernel_call(
        small_body,
        [small_block, small_block],
        [core, innovation, lon_taps, lat_taps, jnp.swapaxes(inv_variance, 0, 1)],
        smem=(0, 4),
        after=(arranged,),
    )
    mate_small = with_mate(sent_small)
    routed, by_lon, by_lat, by_both = kernel_call(
        route_body,
        [shape(3, 3, PIECE, COLS), shape(3, PIECE, COLS), shape(3, PIECE, COLS), shape(PIECE, COLS)],
        [core, longitude, latitude, kept_small, mate_small, obs_tile.reshape(1, -1), obs_cell.reshape(1, -1)],
        smem=(0, 1, 2),
        flops=2 * 72 * slots * obs_tile.shape[0],
    )
    n_lon, n_lat = lax.axis_size("lon"), lax.axis_size("lat")
    opposite = [
        (x * n_lat + y, (x + 2) % n_lon * n_lat + (y + 2) % n_lat)
        for x in range(n_lon)
        for y in range(n_lat)
    ]
    by_lon, by_lat = shifted(by_lon, "lon", 2), shifted(by_lat, "lat", 2)
    by_both = lax.ppermute(by_both, ("lon", "lat"), opposite)
    near, up, down = [jnp.concatenate([routed[i], by_lon[i : i + 1]], axis=0) for i in range(3)]
    far = jnp.concatenate([by_lat, by_both[None]], axis=0)
    first = over_rings(column_call(mix_body, core, columns, vertical, after=(far, near, up, down)))

    def with_rows(strips, rows):
        return jnp.concatenate([strips.reshape(-1, 8, COLS), rows.reshape(-1, 8, COLS)], axis=0)

    before, after = exchanged(
        with_rows(first[6:8], up), with_rows(first[0:2], down), "lat"
    )
    high, low, back_high, back_low, lon_high, lon_low, weight = kernel_call(
        bands_body,
        [shape(planes, ROWS, 128, dtype=BF16)] * 4
        + [shape(planes, COLS, 256, dtype=BF16)] * 2
        + [shape(planes, 1, 128)],
        [core, kept_small, mate_small],
        smem=(0,),
        flops=planes * 200000,
        after=(first,),
    )
    field_shape = shape(planes, ROWS, COLS)
    lat_flops = 2 * 3 * planes * ROWS * 128 * COLS
    row_block = shape(4 * PIECE, COLS)
    pack_rows = shape(nv * PACKED + 4 * PIECE, COLS)
    field, last, lead, own_rows, far_rows = kernel_call(
        functools.partial(lat_body, nv),
        [field_shape, pack_rows, pack_rows, row_block, row_block],
        [latitude, first, before, after, near, far, high, low],
        smem=(0,),
        flops=lat_flops,
    )
    left, right = exchanged(last, lead, "lon")
    pack_shape = shape(nv * PACKED, COLS)
    placed, last, lead = kernel_call(
        functools.partial(observe_body, nv),
        [field_shape, pack_shape, pack_shape],
        [field, left, right, own_rows, far_rows, lon_high, lon_low, weight],
        scratch=[
            pltpu.VMEM((planes, ROWS, 2 * COLS), BF16),
            pltpu.VMEM((planes, 1, slots), F32),
            pltpu.VMEM((planes, 1, slots), F32),
            pltpu.VMEM((planes, 1, slots), F32),
            pltpu.VMEM((ROWS, slots), F32),
            pltpu.VMEM((COLS, slots), BF16),
            pltpu.VMEM((2 * COLS, slots), BF16),
        ],
        flops=2 * planes * ROWS * slots * 256 * 2,
    )
    left, right = exchanged(last, lead, "lon")
    strip_shape = shape(2, planes, 8, COLS)
    back, last, lead = kernel_call(
        functools.partial(back_lon_body, nv),
        [shape(RINGS, planes, 8, COLS), strip_shape, strip_shape],
        [placed, left, right, lon_high, lon_low],
        flops=2 * lat_flops,
    )
    before, after = exchanged(last, lead, "lat")
    back = kernel_call(
        functools.partial(back_lat_body, nv),
        [shape(RINGS, planes, 8, COLS)],
        [latitude, back, before, after, back_high, back_low],
        smem=(0,),
        flops=lat_flops,
    )[0]
    result = over_rings(column_call(unmix_body, core, over_rings(back), vertical, columns))

    mine, other = result[:, :9], with_mate(result[:, 9:])
    return kernel_call(
        finish_body,
        [shape(6, 3, ROWS, COLS)],
        [core, mine, other],
        smem=(0,),
    )[0]


def finish_body(core, mine, other, out):
    c = core[0]
    for v in range(3):
        for l in range(3):
            out[c * 3 + v, l] = mine[:, v * 3 + l].reshape(ROWS, COLS)
            out[(1 - c) * 3 + v, l] = other[:, v * 3 + l].reshape(ROWS, COLS)


def solution(mesh):
    return jax.shard_map(
        local,
        mesh=mesh,
        in_specs=(
            P(None, "lev", "lat", "lon"),
            P(),
            P(None, "lev", None),
            P(None, "lev", None),
            P(None, "lev", ("lon", "lat")),
            P(None, "lev"),
            P(("lon", "lat")),
            P(("lon", "lat")),
        ),
        out_specs=P(None, "lev", "lat", "lon"),
        check_vma=False,
    )
```

```python
import functools

import jax
import jax.numpy as jnp
from jax import lax
from jax.experimental import pallas as pl
from jax.experimental.pallas import tpu as pltpu
from jax.sharding import PartitionSpec as P

F32, BF16, I32 = jnp.float32, jnp.bfloat16, jnp.int32
ROWS, COLS = 64, 128
TAPS = 31
STRIP = 16
LEVELS = 48
RINGS = 8
OWN = 6
SLOTS = 64
TILES = 16
OBS = 512
LON_AT, LAT_AT, WEIGHT_AT, SMALL = OBS, OBS + 128, OBS + 256, OBS + 384
PIECE = 16
VMEM = pl.BlockSpec(memory_space=pltpu.VMEM)
SMEM = pl.BlockSpec(memory_space=pltpu.SMEM)


def kernel_call(body, outs, ins, scratch=(), smem=(), flops=0, limit=16, after=()):
    moved = sum(a.size * a.dtype.itemsize for a in ins)
    moved += sum(o.size * o.dtype.itemsize for o in outs)
    count = len(after)
    return pl.pallas_call(
        lambda *refs: body(*refs[count:]),
        out_shape=list(outs),
        in_specs=[pl.BlockSpec(memory_space=pl.ANY)] * count
        + [SMEM if i in smem else VMEM for i in range(len(ins))],
        out_specs=[VMEM] * len(outs),
        scratch_shapes=list(scratch),
        compiler_params=pltpu.CompilerParams(vmem_limit_bytes=limit * 2**20),
        cost_estimate=pl.CostEstimate(flops=flops, bytes_accessed=moved, transcendentals=0),
    )(*after, *ins)


def shape(*dims, dtype=F32):
    return jax.ShapeDtypeStruct(dims, dtype)


def split(value):
    high = value.astype(BF16)
    return high, (value - high.astype(F32)).astype(BF16)


def mm(a, b):
    return jnp.dot(a, b, preferred_element_type=F32)


def mm_nt(a, b):
    return lax.dot_general(a, b, (((1,), (1,)), ((), ())), preferred_element_type=F32)


def begin_body(core, control, kept, sent):
    c = core[0]
    for which, big in ((c, kept), (1 - c, sent)):
        for v in range(3):
            for l in range(3):
                big[v * 3 + l] = control[which * 3 + v, l]


def small_body(core, innovation, lon_taps, lat_taps, weight, kept, sent):
    c = core[0]
    kept[...] = jnp.zeros(kept.shape, F32)
    sent[...] = jnp.zeros(sent.shape, F32)
    for which, little in ((c, kept), (1 - c, sent)):
        for v in range(3):
            lon, lat, seen = [a[which * 3 + v] for a in (lon_taps, lat_taps, innovation)]
            for l in range(3):
                p = v * 3 + l
                little[p, :, 0:OBS] = seen[l : l + 1]
                little[p, :, LON_AT : LON_AT + TAPS] = lon[l : l + 1]
                little[p, :, LAT_AT : LAT_AT + TAPS] = lat[l : l + 1]
                little[p, :, WEIGHT_AT:] = jnp.full((1, 128), weight[l, which * 3 + v], F32)


def arrange_body(control, mate, out):
    for p in range(9):
        out[:, p] = control[p].reshape(RINGS, 8, COLS)
        out[:, 9 + p] = mate[p].reshape(RINGS, 8, COLS)


def rows_of(v, start, count):
    return pl.ds(v * LEVELS * 8 + start, count)


def mixed(matrix, held, v, side):
    at = [pl.ds(v * LEVELS * 8 + s, LEVELS, stride=8) for s in range(8)]
    columns = jnp.concatenate([held[a, :] for a in at], axis=1)
    (m_high, m_low), (c_high, c_low) = split(matrix.T if side == 0 else matrix), split(columns)
    result = mm(m_high, c_high) + (mm(m_high, c_low) + mm(m_low, c_high))
    for s in range(8):
        held[at[s], :] = result[:, s * COLS : (s + 1) * COLS]


def chip_order(c, part, own, mate):
    return jnp.where(c == part, own, mate)


def mix_body(core, got, matrix, out, held):
    c = core[0]
    for v in range(3):
        for s in range(RINGS):
            own, mate = got[s, v * 3 : v * 3 + 3], got[s, 9 + v * 3 : 12 + v * 3]
            for part in range(2):
                value = chip_order(c, part, own, mate)
                held[rows_of(v, s * 48 + part * 24, 24), :] = value.reshape(24, COLS)
        mixed(matrix[c * 3 + v], held, v, 1)
        for s in range(RINGS):
            out[s, v * OWN : (v + 1) * OWN] = held[rows_of(v, s * 48, 48), :].reshape(OWN, 8, COLS)


def unmix_body(core, got, matrix, control, out, held):
    c = core[0]
    for v in range(3):
        for s in range(RINGS):
            held[rows_of(v, s * 48, 48), :] = got[s, v * OWN : (v + 1) * OWN].reshape(48, COLS)
        mixed(matrix[c * 3 + v], held, v, 0)
        for s in range(RINGS):
            lower, upper = [held[rows_of(v, s * 48 + h * 24, 24), :].reshape(3, 8, COLS) for h in range(2)]
            for t in range(2):
                first = t * 9 + v * 3
                part = chip_order(c, t, lower, upper)
                out[s, first : first + 3] = part + control[s, first : first + 3]


def column_call(body, *ins, after=()):
    return kernel_call(
        body,
        [shape(*ins[1].shape)],
        ins,
        scratch=[pltpu.VMEM((3 * LEVELS * 8, COLS), F32)],
        smem=(0,),
        flops=2 * 3 * LEVELS * LEVELS * 1024 * 6,
        after=after,
    )[0]


def bands_body(core, kept, mate, high, low, back_high, back_low, lon_high, lon_low, weight):
    c = core[0]

    def toeplitz(row, height):
        full = jnp.broadcast_to(row, (height, row.shape[1]))
        return pltpu.roll(full, row.shape[1] - 15, 1, stride=1, stride_axis=0)

    def one(v, carry):
        for l in range(3):
            mine, other = kept[v * 3 + l], mate[v * 3 + l]
            for part in range(2):
                row = jnp.where(c == part, mine, other)
                p = v * OWN + part * 3 + l
                lat = toeplitz(row[:, LAT_AT : LAT_AT + 128], COLS)
                high[p], low[p] = split(lat[:ROWS])
                back_high[p], back_low[p] = split(lat.T[:ROWS])
                lon = jnp.concatenate([row[:, LON_AT : LON_AT + 128], jnp.zeros((1, 128), F32)], axis=1)
                lon_high[p], lon_low[p] = split(toeplitz(lon, COLS))
                weight[p] = row[:, WEIGHT_AT:]
        return carry

    lax.fori_loop(0, 3, one, 0, unroll=True)


def lat_filter(p, rows, before, after, high, low):
    extended = jnp.concatenate(
        [rows[:, p].reshape(ROWS, COLS), after, jnp.zeros((32, COLS), F32), before], axis=0
    )
    e_high, e_low = split(extended)
    return mm(high[p], e_high) + (mm(high[p], e_low) + mm(low[p], e_high))


PACKED = 48


def unpacked(pack, l, base):
    block = pack[l // 2 * STRIP : (l // 2 + 1) * STRIP]
    return jnp.concatenate(
        [
            pltpu.roll(pack, (base - STRIP * l) % COLS, 1) if (base - STRIP * l) % COLS else pack,
            pltpu.roll(block, (base - STRIP * (OWN + l % 2)) % COLS, 1),
        ],
        axis=0,
    )


def with_halo(l, field, left, right):
    lane = lax.broadcasted_iota(I32, (ROWS, COLS), 1)
    left, right = unpacked(left, l, COLS - STRIP), unpacked(right, l, 0)
    halo = jnp.where(lane >= COLS - STRIP, left, jnp.where(lane < STRIP, right, 0.0))
    return split(jnp.concatenate([field, halo], axis=1))


def lon_filter(p, l, field, left, right, high, low):
    x_high, x_low = with_halo(l, field, left, right)
    return mm_nt(x_high, high[p]) + (mm_nt(x_low, high[p]) + mm_nt(x_high, low[p]))


def back_lon_filter(p, l, field, left, right, high, low):
    x_high, x_low = with_halo(l, field, left, right)
    b_high = jnp.concatenate([high[p, :, :COLS], high[p, :, COLS:]], axis=0)
    b_low = jnp.concatenate([low[p, :, :COLS], low[p, :, COLS:]], axis=0)
    return mm(x_high, b_high) + (mm(x_low, b_high) + mm(x_high, b_low))


def packed(fields):
    group = lax.broadcasted_iota(I32, (STRIP, COLS), 1) // STRIP

    def rolled(value, shift):
        return pltpu.roll(value, shift % COLS, 1) if shift % COLS else value

    packs = []
    for base in (COLS - STRIP, 0):
        tops = [rolled(field[:PACKED], STRIP * l - base) for l, field in enumerate(fields)]
        blocks = []
        for i in range(PACKED // STRIP):
            block = tops[0][i * STRIP : (i + 1) * STRIP]
            for l in range(1, OWN):
                block = jnp.where(group == l, tops[l][i * STRIP : (i + 1) * STRIP], block)
            for q in range(2):
                tail = rolled(fields[2 * i + q][PACKED:], STRIP * (OWN + q) - base)
                block = jnp.where(group == OWN + q, tail, block)
            blocks.append(block)
        packs.append(jnp.concatenate(blocks, axis=0))
    return packs


def rows_at(v):
    return pl.ds(pl.multiple_of(v * PACKED, 8), PACKED)


def lat_body(
    nv, latitude, rows, before, after, near, far, high, low, out, last, lead, own_rows, far_rows
):
    y = latitude[0]
    planes = nv * OWN

    def strip(at, p, there):
        both = jnp.concatenate([at[p], at[planes + p]], axis=0)
        return jnp.where(there, both, 0.0)

    def one(v, carry):
        fields = []
        for l in range(OWN):
            p = v * OWN + l
            ends = strip(before, p, y > 0), strip(after, p, y < 3)
            fields.append(lat_filter(p, rows, *ends, high, low))
        for l in range(OWN):
            out[v * OWN + l] = fields[l]
        last[rows_at(v), :], lead[rows_at(v), :] = packed(fields)
        return carry

    lax.fori_loop(0, nv, one, 0, unroll=True)
    for d, (target, block) in enumerate(((own_rows, None), (last, nv), (lead, nv), (far_rows, None))):
        first = 2 * planes + 2 * d
        came = jnp.concatenate(
            [near[d], before[first : first + 2].reshape(PIECE, COLS)]
            + [far[d], after[first : first + 2].reshape(PIECE, COLS)],
            axis=0,
        )
        if block is None:
            target[...] = came
        else:
            target[nv * PACKED :, :] = came


def back_lat_body(nv, latitude, rows, before, after, high, low, out):
    y = latitude[0]

    def one(v, carry):
        for l in range(OWN):
            p = v * OWN + l
            ends = (
                jnp.where(y > 0, before[:, p].reshape(STRIP, COLS), 0.0),
                jnp.where(y < 3, after[:, p].reshape(STRIP, COLS), 0.0),
            )
            out[:, p] = lat_filter(p, rows, *ends, high, low).reshape(RINGS, 8, COLS)
        return carry

    lax.fori_loop(0, nv, one, 0, unroll=True)


def back_lon_body(nv, field, left, right, high, low, out, last, lead):
    def one(v, carry):
        for l in range(OWN):
            p = v * OWN + l
            value = back_lon_filter(p, l, field[p], left[rows_at(v), :], right[rows_at(v), :], high, low)
            out[:, p] = value.reshape(RINGS, 8, COLS)
            last[:, p] = value[ROWS - STRIP :].reshape(2, 8, COLS)
            lead[:, p] = value[:STRIP].reshape(2, 8, COLS)
        return carry

    lax.fori_loop(0, nv, one, 0, unroll=True)


def observe_body(
    nv, field, left, right, own_rows, far_rows, high, low, weight,
    out, last, first, parts, values, misfit_high, misfit_low, row_hot, col_hot, col_hot2,
):
    came = pl.ds(nv * PACKED, 4 * PIECE)
    blocks = [own_rows[...], left[came, :], far_rows[...], right[came, :]]
    arrived(blocks, values, row_hot, col_hot, col_hot2)

    def filtered(v, carry):
        for l in range(OWN):
            p = v * OWN + l
            third = lon_filter(p, l, field[p], left[rows_at(v), :], right[rows_at(v), :], high, low)
            t_high, t_low = split(third)
            parts[p] = jnp.concatenate([t_high, t_low], axis=1)
        return carry

    lax.fori_loop(0, nv, filtered, 0, unroll=True)

    def gathered(v, carry):
        block = parts[pl.ds(v * OWN, OWN)].reshape(OWN * ROWS, 2 * COLS)
        across = mm(block, col_hot2[...])
        for l in range(OWN):
            p = v * OWN + l
            found = jnp.sum(across[l * ROWS : (l + 1) * ROWS] * row_hot[...], axis=0, keepdims=True)
            misfit = (found - values[p]) * jnp.concatenate([weight[p]] * 8, axis=1)
            m_high, m_low = split(misfit)
            misfit_high[p] = m_high.astype(F32)
            misfit_low[p] = m_low.astype(F32)
        return carry

    lax.fori_loop(0, nv, gathered, 0, unroll=True)

    def scattered(v, carry):
        placed = []
        for l in range(OWN):
            p = v * OWN + l
            placed.append((row_hot[...] * misfit_high[p]).astype(BF16))
            placed.append((row_hot[...] * misfit_low[p]).astype(BF16))
        both = mm_nt(jnp.concatenate(placed, axis=0), col_hot[...])
        fields = []
        for l in range(OWN):
            at = 2 * l * ROWS
            fields.append(both[at : at + ROWS] + both[at + ROWS : at + 2 * ROWS])
            out[v * OWN + l] = fields[-1]
        last[rows_at(v), :], first[rows_at(v), :] = packed(fields)
        return carry

    lax.fori_loop(0, nv, scattered, 0, unroll=True)


def route_body(core, longitude, latitude, kept, mate, tile, cell, out, by_lon, by_lat, by_both):
    c = core[0]
    count = tile.shape[1]
    east = ((tile[...] >> 2) - longitude[0]) & 3
    north = ((tile[...] & 3) - latitude[0]) & 3
    away = north * 4 + east
    hot = (lax.broadcasted_iota(I32, (TILES, count), 0) == away).astype(F32)
    earlier = lax.broadcasted_iota(I32, (count, count), 0) < lax.broadcasted_iota(I32, (count, count), 1)
    before = mm(hot.astype(BF16), earlier.astype(F32).astype(BF16))
    place = jnp.sum(before * hot, axis=0, keepdims=True).astype(I32)
    slot = away * SLOTS + place
    slot_hot = (lax.broadcasted_iota(I32, (TILES * SLOTS, count), 0) == slot).astype(F32).astype(BF16)
    observed = []
    for v in range(3):
        for part in range(2):
            for l in range(3):
                p = v * 3 + l
                observed.append(jnp.where(c == part, kept[p, :, 0:OBS], mate[p, :, 0:OBS]))
    sent = jnp.concatenate(
        observed + [(cell[...] + 1).astype(F32), jnp.zeros((5, count), F32)], axis=0
    )
    high, rest = split(sent)
    remainder = sent - high.astype(F32)
    low = (remainder - rest.astype(F32)).astype(BF16)
    all_parts = mm_nt(jnp.concatenate([high, rest, low], axis=0), slot_hot)
    full = all_parts[0:24] + (all_parts[24:48] + all_parts[48:72])
    lane = lax.broadcasted_iota(I32, (8, COLS), 1)
    for e in range(TILES // 2):
        at = slice(e * COLS, (e + 1) * COLS)
        a, b, c = full[0:8, at], full[8:16, at], full[16:24, at]
        a2, b2, c2 = [pltpu.roll(x, SLOTS, 1) for x in (a, b, c)]
        pair = (
            (jnp.where(lane < SLOTS, a, b2), jnp.where(lane < SLOTS, c, 0.0)),
            (jnp.where(lane < SLOTS, a2, b), jnp.where(lane < SLOTS, c2, 0.0)),
        )
        for i in range(2):
            north, east = e // 2, e % 2 * 2 + i
            y, x = (0, 1, None, 2)[north], (0, 1, None, 2)[east]
            if x is None:
                target = by_both if y is None else by_lon.at[y]
            else:
                target = by_lat.at[x] if y is None else out.at[y, x]
            target[0:8], target[8:16] = pair[i]


def arrived(blocks, values, row_hot, col_hot, col_hot2):
    low = lax.broadcasted_iota(I32, (8, COLS), 1) < SLOTS
    full = []
    for block in blocks:
        for first in (0, 2 * PIECE):
            a, c, b, d = [block[first + 8 * i : first + 8 * i + 8] for i in range(4)]
            full.append(
                jnp.concatenate(
                    [
                        jnp.where(low, a, pltpu.roll(b, SLOTS, 1)),
                        jnp.where(low, pltpu.roll(a, SLOTS, 1), b),
                        jnp.where(low, c, pltpu.roll(d, SLOTS, 1)),
                    ],
                    axis=0,
                )
            )
    full = jnp.concatenate(full, axis=1)
    for p in range(18):
        values[p] = full[p : p + 1]
    cell = full[18:19].astype(I32) - 1
    count = cell.shape[1]
    row_hot[...] = (lax.broadcasted_iota(I32, (ROWS, count), 0) == (cell >> 7)).astype(F32)
    cols = (lax.broadcasted_iota(I32, (COLS, count), 0) == (cell & 127)).astype(F32).astype(BF16)
    col_hot[...] = cols
    col_hot2[0:COLS] = cols
    col_hot2[COLS : 2 * COLS] = cols


def exchanged(last, first, axis):
    size = lax.axis_size(axis)
    up = [(i, (i + 1) % size) for i in range(size)]
    down = [(j, i) for i, j in up]
    return lax.ppermute(last, axis, up), lax.ppermute(first, axis, down)


def shifted(value, axis, by):
    size = lax.axis_size(axis)
    return lax.ppermute(value, axis, [(i, (i + by) % size) for i in range(size)])


def with_mate(value):
    pairs = [(i, i ^ 1) for i in range(lax.axis_size("lev"))]
    return lax.ppermute(value, "lev", pairs)


def over_rings(value):
    size = lax.axis_size("lev")
    groups = [list(range(0, size, 2)), list(range(1, size, 2))]
    return lax.all_to_all(value, "lev", 0, 0, tiled=True, axis_index_groups=groups)


def local(control, vertical, lon_taps, lat_taps, innovation, inv_variance, obs_tile, obs_cell):
    def index(axis):
        return lax.axis_index(axis).astype(I32).reshape(1)

    core, longitude, latitude = index("lev") % 2, index("lon"), index("lat")
    nv = 3
    planes = nv * OWN
    slots = TILES * SLOTS

    block, small_block = shape(9, ROWS, COLS), shape(9, 1, SMALL)
    kept, sent = kernel_call(begin_body, [block, block], [core, control], smem=(0,))
    arranged = kernel_call(
        arrange_body, [shape(RINGS, planes, 8, COLS)], [kept, with_mate(sent)]
    )[0]
    columns = over_rings(arranged)

    kept_small, sent_small = kernel_call(
        small_body,
        [small_block, small_block],
        [core, innovation, lon_taps, lat_taps, jnp.swapaxes(inv_variance, 0, 1)],
        smem=(0, 4),
        after=(arranged,),
    )
    mate_small = with_mate(sent_small)
    routed, by_lon, by_lat, by_both = kernel_call(
        route_body,
        [shape(3, 3, PIECE, COLS), shape(3, PIECE, COLS), shape(3, PIECE, COLS), shape(PIECE, COLS)],
        [core, longitude, latitude, kept_small, mate_small, obs_tile.reshape(1, -1), obs_cell.reshape(1, -1)],
        smem=(0, 1, 2),
        flops=2 * 72 * slots * obs_tile.shape[0],
    )
    n_lon, n_lat = lax.axis_size("lon"), lax.axis_size("lat")
    opposite = [
        (x * n_lat + y, (x + 2) % n_lon * n_lat + (y + 2) % n_lat)
        for x in range(n_lon)
        for y in range(n_lat)
    ]
    by_lon, by_lat = shifted(by_lon, "lon", 2), shifted(by_lat, "lat", 2)
    by_both = lax.ppermute(by_both, ("lon", "lat"), opposite)
    near, up, down = [jnp.concatenate([routed[i], by_lon[i : i + 1]], axis=0) for i in range(3)]
    far = jnp.concatenate([by_lat, by_both[None]], axis=0)
    first = over_rings(column_call(mix_body, core, columns, vertical, after=(far, near, up, down)))

    def with_rows(strips, rows):
        return jnp.concatenate([strips.reshape(-1, 8, COLS), rows.reshape(-1, 8, COLS)], axis=0)

    before, after = exchanged(
        with_rows(first[6:8], up), with_rows(first[0:2], down), "lat"
    )
    high, low, back_high, back_low, lon_high, lon_low, weight = kernel_call(
        bands_body,
        [shape(planes, ROWS, 128, dtype=BF16)] * 4
        + [shape(planes, COLS, 256, dtype=BF16)] * 2
        + [shape(planes, 1, 128)],
        [core, kept_small, mate_small],
        smem=(0,),
        flops=planes * 200000,
        after=(first,),
    )
    field_shape = shape(planes, ROWS, COLS)
    lat_flops = 2 * 3 * planes * ROWS * 128 * COLS
    row_block = shape(4 * PIECE, COLS)
    pack_rows = shape(nv * PACKED + 4 * PIECE, COLS)
    field, last, lead, own_rows, far_rows = kernel_call(
        functools.partial(lat_body, nv),
        [field_shape, pack_rows, pack_rows, row_block, row_block],
        [latitude, first, before, after, near, far, high, low],
        smem=(0,),
        flops=lat_flops,
    )
    left, right = exchanged(last, lead, "lon")
    pack_shape = shape(nv * PACKED, COLS)
    placed, last, lead = kernel_call(
        functools.partial(observe_body, nv),
        [field_shape, pack_shape, pack_shape],
        [field, left, right, own_rows, far_rows, lon_high, lon_low, weight],
        scratch=[
            pltpu.VMEM((planes, ROWS, 2 * COLS), BF16),
            pltpu.VMEM((planes, 1, slots), F32),
            pltpu.VMEM((planes, 1, slots), F32),
            pltpu.VMEM((planes, 1, slots), F32),
            pltpu.VMEM((ROWS, slots), F32),
            pltpu.VMEM((COLS, slots), BF16),
            pltpu.VMEM((2 * COLS, slots), BF16),
        ],
        flops=2 * planes * ROWS * slots * 256 * 2,
    )
    left, right = exchanged(last, lead, "lon")
    strip_shape = shape(2, planes, 8, COLS)
    back, last, lead = kernel_call(
        functools.partial(back_lon_body, nv),
        [shape(RINGS, planes, 8, COLS), strip_shape, strip_shape],
        [placed, left, right, lon_high, lon_low],
        flops=2 * lat_flops,
    )
    before, after = exchanged(last, lead, "lat")
    back = kernel_call(
        functools.partial(back_lat_body, nv),
        [shape(RINGS, planes, 8, COLS)],
        [latitude, back, before, after, back_high, back_low],
        smem=(0,),
        flops=lat_flops,
    )[0]
    result = over_rings(column_call(unmix_body, core, over_rings(back), vertical, columns))

    other = with_mate(result[:, 9:])
    return kernel_call(
        finish_body,
        [shape(6, 3, ROWS, COLS)],
        [core, result, other],
        smem=(0,),
    )[0]


def finish_body(core, mine, other, out):
    c = core[0]
    for v in range(3):
        for l in range(3):
            out[c * 3 + v, l] = mine[:, v * 3 + l].reshape(ROWS, COLS)
            out[(1 - c) * 3 + v, l] = other[:, v * 3 + l].reshape(ROWS, COLS)


def solution(mesh):
    return jax.shard_map(
        local,
        mesh=mesh,
        in_specs=(
            P(None, "lev", "lat", "lon"),
            P(),
            P(None, "lev", None),
            P(None, "lev", None),
            P(None, "lev", ("lon", "lat")),
            P(None, "lev"),
            P(("lon", "lat")),
            P(("lon", "lat")),
        ),
        out_specs=P(None, "lev", "lat", "lon"),
        check_vma=False,
    )
```
